128 devices in a mesh: dp: 8 (over z, core), proto: 16 (over x, y).
Axes of the slice: x: 4, y: 4, z: 4, core: 2. Of those that a mesh axis runs over, the one named last changes fastest.
Arguments:
- student_in: bfloat16 [4096, 1536], P(('dp', 'proto')), may hold values from -10 to 10
- teacher_in: bfloat16 [4096, 1536], P(('dp', 'proto')), may hold values from -10 to 10
- w1_student: bfloat16 [1536, 2048], P(None, 'proto'), may hold values from -0.15625 to 0.15625
- w2_student: bfloat16 [2048, 256], P('proto'), may hold values from -0.125 to 0.125
- w1_teacher: bfloat16 [1536, 2048], P(None, 'proto'), may hold values from -0.15625 to 0.15625
- w2_teacher: bfloat16 [2048, 256], P('proto'), may hold values from -0.125 to 0.125
- prototypes: bfloat16 [131072, 256], P(('dp', 'proto')), may hold values from -0.25 to 0.25
Outputs:
- grad_proto: float32 [131072, 256], P(('dp', 'proto'))
- grad_w1: float32 [1536, 2048], P(None, 'proto')
- grad_w2: float32 [2048, 256], P('proto')
- loss: float32 [], replicated
The draws below stay inside these ranges and needn't reach their ends.
All inputs are finite; a program needn't handle non-finite values.
Results may differ from the reference program's by a relative error of at most 0.0008.
Values may be sent and summed in bfloat16 or wider, within the bound.
A program may use at most 128 MiB of HBM per device.

```python
import math
import jax
import jax.numpy as jnp
from jax import lax

E = 1536
H = 2048
C = 256
K = 131072
ITERS = 3
VIEW_COUNT = 4096
GROUP_ROWS = 512
N_DP = 8
N_PROTO = 16


def group_common(key):
    common = jnp.clip(jax.random.normal(key, (N_DP, E), jnp.float32), -2.0, 2.0)
    groups = jnp.arange(VIEW_COUNT, dtype=jnp.int32) // GROUP_ROWS
    picked = (groups[:, None] == jnp.arange(N_DP, dtype=jnp.int32)[None, :]).astype(jnp.float32)
    rank = groups.astype(jnp.float32) / max(N_DP - 1, 1)
    return (jnp.dot(picked, common, precision=jax.lax.Precision.HIGHEST), rank)


def crop_rows(key, fold):
    shared, rank = group_common(key)
    key = jax.random.fold_in(key, fold)
    noise = jnp.clip(jax.random.normal(key, (VIEW_COUNT, E), jnp.float32), -3.0, 3.0)
    weight = 0.8 + 1.6 * rank
    return (shared * weight[:, None] + noise).astype(jnp.bfloat16)


def draw_student_in(key, part):
    return crop_rows(key, 21)


def draw_teacher_in(key, part):
    return crop_rows(key, 23)


def draw_prototypes(key, part):
    key = jax.random.fold_in(key, 11)
    first_key = jax.random.fold_in(key, 0)
    third_key = jax.random.fold_in(key, 2)
    noise = jnp.clip(jax.random.normal(first_key, (K, C), jnp.float32), -2.0, 2.0)
    shard_dirs = jnp.clip(jax.random.normal(third_key, (N_PROTO, C), jnp.float32), -1.3, 1.3)
    block = jnp.arange(K, dtype=jnp.int32) // (K // (N_DP * N_PROTO))
    shard = block % N_PROTO
    picked = (shard[:, None] == jnp.arange(N_PROTO, dtype=jnp.int32)[None, :]).astype(jnp.float32)
    rank = jnp.arange(N_PROTO, dtype=jnp.float32) / max(N_PROTO - 1, 1)
    weighted = shard_dirs * (0.5 + rank)[:, None]
    values = (noise + jnp.dot(picked, weighted, precision=jax.lax.Precision.HIGHEST)) / math.sqrt(C)
    return values.astype(jnp.bfloat16)


def shard_levels(stream_key, extent, cuts, smallest, high):
    gain = 1.0
    for dim, shards_of in cuts:
        draws = jax.random.uniform(jax.random.fold_in(jax.random.fold_in(stream_key, 6), dim), (shards_of,), jnp.float32, smallest / len(cuts), high / len(cuts))
        gain = gain * jnp.repeat(jnp.exp(draws), extent[dim] // shards_of).reshape((-1,) + (1,) * (len(extent) - 1 - dim))
    return gain


def scatter_about(stream_key, dims, deviation, limit, cuts=(), held_as=jnp.bfloat16):
    level = shard_levels(stream_key, dims, cuts, -0.22, 0.18) if cuts else 1.0
    values = jax.random.normal(stream_key, dims, jnp.float32) * deviation * level
    return jnp.minimum(jnp.maximum(values, -limit), limit).astype(held_as)


def setup_inputs(seed: int = 0) -> dict:
    key_list = jax.random.split(jax.random.key(seed), 8)
    student_in = draw_student_in(jax.random.fold_in(key_list[7], 71), 0)
    teacher_in = draw_teacher_in(jax.random.fold_in(key_list[7], 71), 0)
    w1_student = scatter_about(key_list[2], (E, H), E ** -0.5, 0.15625, ((1, 16),))
    w2_student = scatter_about(key_list[3], (H, C), H ** -0.5, 0.125, ((0, 16),))
    w1_teacher = scatter_about(key_list[4], (E, H), E ** -0.5, 0.15625, ((1, 16),))
    w2_teacher = scatter_about(key_list[5], (H, C), H ** -0.5, 0.125, ((0, 16),))
    prototypes = draw_prototypes(jax.random.fold_in(key_list[7], 71), 0)
    return {"student_in": student_in, "teacher_in": teacher_in, "w1_student": w1_student, "w2_student": w2_student, "w1_teacher": w1_teacher, "w2_teacher": w2_teacher, "prototypes": prototypes}


teacher_temp = 0.07
learner_sharpness = 0.1

def gelu_exact(values):
    return jax.nn.gelu(values, approximate=False)

def head_rows(rows_in, w_first, second_weight):
    pre = jnp.dot(rows_in, w_first, preferred_element_type=jnp.float32)
    hidden = gelu_exact(pre).astype(jnp.bfloat16)
    raw = jnp.dot(hidden, second_weight, preferred_element_type=jnp.float32)
    scale = lax.rsqrt(lax.optimization_barrier(jnp.sum(raw * raw, axis=1, keepdims=True)) + 1e-06)
    return (pre, hidden, raw * scale, scale)

def slab_scores(unit, slab_index, temp):
    return jnp.dot(unit, slab_index.T, preferred_element_type=jnp.float32) / temp

def partial_scale(column_scale, weight_row):

    def apply_block(slab_index):
        return column_scale(slab_index, weight_row)
    return apply_block

def reference(student_in, teacher_in, w1_student, w2_student, w1_teacher, w2_teacher, prototypes):
    stud_pre, stud_hidden, stud_float, stud_scale = head_rows(student_in, w1_student, w2_student)
    _, _, teach_float, _ = head_rows(teacher_in, w1_teacher, w2_teacher)
    learner_direction = stud_float.astype(jnp.bfloat16)
    teach_unit = teach_float.astype(jnp.bfloat16)
    blocks = prototypes.reshape(N_DP * N_PROTO, -1, C)
    crop_count = learner_direction.shape[0]

    def teach_exp(slab_index):
        return jnp.exp(slab_scores(teach_unit, slab_index, teacher_temp))

    def column_scale(slab_index, weight_row):
        return 1.0 / (K * lax.optimization_barrier(jnp.sum(teach_exp(slab_index) * weight_row[:, None], axis=0)))

    def row_add(running_state, pair):
        slab_index, scales = pair
        return (running_state + lax.optimization_barrier(jnp.sum(teach_exp(slab_index) * scales[None, :], axis=1)), None)
    weight_row = jnp.ones((crop_count,), jnp.float32)
    for sweep in range(ITERS):
        col_scale = lax.map(partial_scale(column_scale, weight_row), blocks)
        row_sum, _ = lax.scan(row_add, jnp.zeros((crop_count,), jnp.float32), (blocks, col_scale))
        weight_row = 1.0 / (VIEW_COUNT * row_sum)

    def student_add(running_state, slab_index):
        return (running_state + lax.optimization_barrier(jnp.sum(jnp.exp(slab_scores(learner_direction, slab_index, learner_sharpness)), axis=1)), None)
    stud_total, _ = lax.scan(student_add, jnp.zeros((crop_count,), jnp.float32), blocks)
    log_norm = jnp.log(stud_total)

    def finish(running_state, pair):
        slab_index, scales = pair
        assignment_labels = teach_exp(slab_index) * scales[None, :] / row_sum[:, None]
        learner_score = slab_scores(learner_direction, slab_index, learner_sharpness)
        learner_softmax = jnp.exp(learner_score - log_norm[:, None])
        score_derivative = ((learner_softmax - assignment_labels) / (VIEW_COUNT * learner_sharpness)).astype(jnp.bfloat16)
        partial_loss = jnp.sum(assignment_labels * (log_norm[:, None] - learner_score))
        normalized_gradient = running_state[0] + jnp.dot(score_derivative, slab_index, preferred_element_type=jnp.float32)
        proto_grad = jnp.dot(score_derivative.T, learner_direction, preferred_element_type=jnp.float32)
        return ((normalized_gradient, running_state[1] + partial_loss), proto_grad)
    start_carry = (jnp.zeros((crop_count, C), jnp.float32), jnp.zeros((), jnp.float32))
    (normalized_gradient, loss_accumulated), proto_grads = lax.scan(finish, start_carry, (blocks, col_scale))
    grad_proto = proto_grads.reshape(K, C)
    loss = loss_accumulated / VIEW_COUNT
    along = lax.optimization_barrier(jnp.sum(stud_float * normalized_gradient, axis=1, keepdims=True))
    raw_grad = ((normalized_gradient - stud_float * along) * stud_scale).astype(jnp.bfloat16)
    grad_w2 = jnp.dot(stud_hidden.T, raw_grad, preferred_element_type=jnp.float32)
    hidden_grad = jnp.dot(raw_grad, w2_student.T, preferred_element_type=jnp.float32)
    _, backward = jax.vjp(gelu_exact, stud_pre)
    pre_grad = backward(hidden_grad)[0].astype(jnp.bfloat16)
    grad_w1 = jnp.dot(student_in.T, pre_grad, preferred_element_type=jnp.float32)
    return (grad_proto, grad_w1, grad_w2, loss)
```

```python
import functools
import math

import jax
import jax.numpy as jnp
from jax import lax
from jax.experimental import pallas as pl
from jax.experimental.pallas import tpu as pltpu
from jax.sharding import PartitionSpec as P

MESH = pl.DeviceIdType.MESH
TEACHER_TEMP = 0.07
STUDENT_TEMP = 0.1
LOG2E = 1.4426950408889634
LN2 = 0.6931471805599453
F32 = jnp.float32
BF16 = jnp.bfloat16


def normal_cdf(x):
    return 0.5 * (1.0 + lax.erf(x * (1.0 / math.sqrt(2.0))))


def gelu(x):
    return x * normal_cdf(x)


def gelu_slope(x):
    return normal_cdf(x) + x * (jnp.exp(-0.5 * x * x) * (1.0 / math.sqrt(2.0 * math.pi)))


def nt_dot(a, b):
    return lax.dot_general(a, b, (((1,), (1,)), ((), ())), preferred_element_type=F32)


def tn_dot(a, b):
    return lax.dot_general(a, b, (((0,), (0,)), ((), ())), preferred_element_type=F32)


def unit_scale(raw):
    return lax.rsqrt(jnp.sum(raw * raw, axis=1, keepdims=True) + 1e-06)


class Sems:
    def __init__(self):
        self.count = 0

    def take(self, n):
        base = self.count
        self.count += n
        return base


def kernel(dims, plan, s_in, t_in, w1s, w2s, w1t, w2t, protos, gp_out, gw1_out, gw2_out, loss_out, *scratch):
    nz, nx, ny, rb, q = dims["nz"], dims["nx"], dims["ny"], dims["rb"], dims["q"]
    ndp, npr = 2 * nz, nx * ny
    width, hb, cols, kp = w1s.shape[0], w1s.shape[1], w2s.shape[1], protos.shape[0]
    group = rb * npr
    crops = group * ndp
    total_protos = kp * ndp * npr
    tiles = crops // 128
    half = cols // 2
    (tok, pre_s, hid_s, rawp, rawr, unit, own_float, own_scale, ex, lg2, colb, wb, rows8, ps1, psa, psb, psbr, psc,
     gt, ptr, ugt, sibs, sibr, part, zrecv, precv, a2, a2r, b2, b2r, losst, lossr, lossd, lossdr, rg,
     gw, gwr, gwz, fw, ssem, rsem) = scratch
    units = unit

    dp, me = lax.axis_index("dp"), lax.axis_index("proto")
    z, c = dp // 2, dp % 2
    x, y = me // ny, me % ny

    def started(src, dst, sem, to_dp, to_proto):
        pltpu.make_async_remote_copy(
            src_ref=src, dst_ref=dst, send_sem=ssem.at[sem], recv_sem=rsem.at[sem],
            device_id=(to_dp, to_proto), device_id_type=MESH,
        ).start()

    def arrived(dst, sem):
        pltpu.make_async_copy(dst, dst, rsem.at[sem]).wait()

    def gone(src, sem):
        pltpu.make_async_copy(src, src, ssem.at[sem]).wait()

    def loop(lo, hi, fn):
        def step(k, carry):
            fn(k)
            return carry

        lax.fori_loop(lo, hi, step, 0)

    def proto_of(xx, yy):
        return lax.rem(xx + nx, nx) * ny + lax.rem(yy + ny, ny)

    def rows(p):
        return pl.ds(pl.multiple_of(p * rb, rb), rb)

    def ring(value, n):
        return lax.rem(value + n, n)

    barrier = pltpu.get_barrier_semaphore()

    def greet_proto(k):
        pl.semaphore_signal(barrier, inc=1, device_id=(dp, ring(me + k, npr)), device_id_type=MESH)

    def greet_dp(k):
        pl.semaphore_signal(barrier, inc=1, device_id=(ring(dp + k, ndp), me), device_id_type=MESH)

    loop(1, npr, greet_proto)
    loop(1, ndp, greet_dp)
    pl.semaphore_wait(barrier, npr - 1 + ndp - 1)

    inputs = (t_in, s_in)
    w1_of, w2_of = (w1t, w1s), (w2t, w2s)
    left, right = pl.ds(0, width // 2), pl.ds(width // 2, width // 2)
    lo, hi = pl.ds(0, half), pl.ds(half, half)
    sib = dp + 1 - 2 * c

    def tokens_start(v):
        tok[v, rows(me), :] = inputs[v][...]
        for k in range(1, nx):
            started(tok.at[v, rows(me)], tok.at[v, rows(me)], plan["tx"][v] + k, dp, proto_of(x + k, y))
        for k in range(1, ny):
            started(tok.at[v, rows(me)], tok.at[v, rows(me)], plan["ty"][v] + k, dp, proto_of(x, y + k))

    def tokens_forward(v):
        for k in range(1, max(nx, ny)):
            if k < nx:
                block = rows(proto_of(x - k, y))
                arrived(tok.at[v, block], plan["tx"][v] + k)
                for m in range(1, ny):
                    ref = tok.at[v, block, left]
                    started(ref, ref, plan["fa"][v] + k * ny + m, dp, proto_of(x, y + m))
            if k < ny:
                block = rows(proto_of(x, y - k))
                arrived(tok.at[v, block], plan["ty"][v] + k)
                for m in range(1, nx):
                    ref = tok.at[v, block, right]
                    started(ref, ref, plan["fb"][v] + k * nx + m, dp, proto_of(x + m, y))

    def tokens_wait(v):
        for k in range(1, nx):
            for m in range(1, ny):
                arrived(tok.at[v, rows(proto_of(x - k, y - m)), left], plan["fa"][v] + k * ny + m)
        for k in range(1, ny):
            for m in range(1, nx):
                arrived(tok.at[v, rows(proto_of(x - m, y - k)), right], plan["fb"][v] + k * nx + m)

    def tokens_drain(v):
        for k in range(1, nx):
            gone(tok.at[v, rows(me)], plan["tx"][v] + k)
            for m in range(1, ny):
                gone(tok.at[v, rows(proto_of(x - k, y)), left], plan["fa"][v] + k * ny + m)
        for k in range(1, ny):
            gone(tok.at[v, rows(me)], plan["ty"][v] + k)
            for m in range(1, nx):
                gone(tok.at[v, rows(proto_of(x, y - k)), right], plan["fb"][v] + k * nx + m)

    def head(v):
        step = min(group, 128)

        def chunk(i):
            r = pl.ds(pl.multiple_of(i * step, step), step)
            pre = jnp.dot(tok[v, r, :], w1_of[v][...], preferred_element_type=F32)
            hidden = gelu(pre).astype(BF16)
            if v == 1:
                pre_s[r, :] = pre
                hid_s[r, :] = hidden
            rawp[v, r, :] = jnp.dot(hidden, w2_of[v][...], preferred_element_type=F32)

        loop(0, group // step, chunk)

    def raw_send(v):
        def send(k):
            to = ring(me + k, npr)
            started(rawp.at[v, rows(to)], rawr.at[v, k], plan["rr"][v] + k, dp, to)

        loop(1, npr, send)

    def raw_finish(v):
        loop(1, npr, lambda k: arrived(rawr.at[v, k], plan["rr"][v] + k))
        raw = lax.fori_loop(1, npr, lambda k, s: s + rawr[v, k], rawp[v, rows(me), :])
        scale = unit_scale(raw)
        unit_float = raw * scale
        if v == 1:
            own_float[...] = unit_float
            own_scale[...] = scale
        units[v, z, c, rows(me), :] = unit_float.astype(BF16)

    def raw_drain(v):
        loop(1, npr, lambda k: gone(rawp.at[v, rows(ring(me + k, npr))], plan["rr"][v] + k))

    def ag_first(v):
        mine = units.at[v, z, c, rows(me)]
        loop(1, npr, lambda k: started(mine.at[:, lo], mine.at[:, lo], plan["a1"][v] + k, dp, ring(me + k, npr)))
        for k in range(1, nz):
            started(mine.at[:, hi], mine.at[:, hi], plan["b1"][v] + k, ring(z + k, nz) * 2 + c, me)

    def ag_second(v):
        for k in range(1, nz):
            arrived(units.at[v, ring(z - k, nz), c, rows(me), hi], plan["b1"][v] + k)
        col = units.at[v, :, c, rows(me), hi]
        loop(1, npr, lambda k: started(col, col, plan["b2"][v] + k, dp, ring(me + k, npr)))
        loop(1, npr, lambda k: arrived(units.at[v, z, c, rows(ring(me - k, npr)), lo], plan["a1"][v] + k))
        plane = units.at[v, z, c, :, lo]
        for k in range(1, nz):
            started(plane, plane, plan["a2"][v] + k, ring(z + k, nz) * 2 + c, me)
        started(plane, plane, plan["sa"][v], sib, me)

    def ag_third(v):
        for k in range(1, nz):
            plane = units.at[v, ring(z - k, nz), c, :, lo]
            arrived(plane, plan["a2"][v] + k)
            started(plane, plane, plan["sa"][v] + k, sib, me)
        loop(1, npr, lambda k: arrived(units.at[v, :, c, rows(ring(me - k, npr)), hi], plan["b2"][v] + k))
        whole = units.at[v, :, c, :, hi]
        started(whole, whole, plan["sb"][v], sib, me)

    def ag_wait(v):
        for k in range(nz):
            arrived(units.at[v, ring(z - k, nz), 1 - c, :, lo], plan["sa"][v] + k)
        arrived(units.at[v, :, 1 - c, :, hi], plan["sb"][v])

    def ag_drain(v):
        mine = units.at[v, z, c, rows(me)]
        loop(1, npr, lambda k: gone(mine.at[:, lo], plan["a1"][v] + k))
        loop(1, npr, lambda k: gone(units.at[v, :, c, rows(me), hi], plan["b2"][v] + k))
        for k in range(1, nz):
            gone(mine.at[:, hi], plan["b1"][v] + k)
            gone(units.at[v, z, c, :, lo], plan["a2"][v] + k)
        for k in range(nz):
            gone(units.at[v, ring(z - k, nz), c, :, lo], plan["sa"][v] + k)
        gone(units.at[v, :, c, :, hi], plan["sb"][v])

    pb = min(kp, 256)
    gtiles = group // 128

    def teacher_scores():
        colb[...] = jnp.zeros_like(colb)

        def step(i):
            g, b = i // (kp // pb), i % (kp // pb)
            r = pl.ds(pl.multiple_of(b * pb, pb), pb)
            s = nt_dot(protos[r, :], units[0, g // 2, g % 2])
            e = jnp.exp2(s * (LOG2E / TEACHER_TEMP))
            ex[r, pl.ds(pl.multiple_of(g * group, group), group)] = e
            acc = e[:, :128]
            for j in range(1, gtiles):
                acc = acc + e[:, j * 128 : (j + 1) * 128]
            colb[r, :] += acc

        loop(0, ndp * (kp // pb), step)

        def scale(i):
            r = pl.ds(pl.multiple_of(i * 64, 64), 64)
            total = jnp.sum(colb[r, :], axis=1, keepdims=True)
            colb[r, :] = jnp.broadcast_to(1.0 / (total_protos * total), (64, 128))

        loop(0, kp // 64, scale)

    def student_scores():
        rows8[...] = jnp.zeros_like(rows8)

        def step(i):
            g, b = i // (kp // pb), i % (kp // pb)
            r = pl.ds(pl.multiple_of(b * pb, pb), pb)
            cc = pl.ds(pl.multiple_of(g * group, group), group)
            s = nt_dot(protos[r, :], units[1, g // 2, g % 2]) * (LOG2E / STUDENT_TEMP)
            lg2[r, cc] = s
            e = jnp.exp2(s)
            rows8[:, cc] += jnp.sum(e.reshape(pb // 8, 8, group), axis=0)

        loop(0, ndp * (kp // pb), step)

    def row_pass(fresh):
        rows8[...] = jnp.zeros_like(rows8)

        def step(i):
            base = pl.multiple_of(i * 64, 64)
            if fresh:
                accs = [None] * 8
                for j in range(tiles):
                    lanes = slice(j * 128, (j + 1) * 128)
                    w = wb[0:8, lanes]
                    for a in range(8):
                        term = ex[pl.ds(base + 8 * a, 8), lanes] * w
                        accs[a] = term if accs[a] is None else accs[a] + term
                scales = []
                for a in range(8):
                    total = jnp.sum(accs[a], axis=1, keepdims=True)
                    scale = jnp.broadcast_to(1.0 / (total_protos * total), (8, 128))
                    colb[pl.ds(base + 8 * a, 8), :] = scale
                    scales.append(scale)
            else:
                scales = [colb[pl.ds(base + 8 * a, 8), :] for a in range(8)]
            for j in range(tiles):
                lanes = slice(j * 128, (j + 1) * 128)
                terms = [ex[pl.ds(base + 8 * a, 8), lanes] * scales[a] for a in range(8)]
                while len(terms) > 1:
                    terms = [terms[n] + terms[n + 1] for n in range(0, len(terms), 2)]
                rows8[:, lanes] += terms[0]

        loop(0, kp // 64, step)

    def put_rows(t, at):
        for j in range(tiles):
            ps1[t, j // q, at + j % q : at + j % q + 1, :] = jnp.sum(
                rows8[:, j * 128 : (j + 1) * 128], axis=0, keepdims=True
            )

    def sum_send(t):
        def send(k):
            to = ring(dp + k, ndp)
            started(ps1.at[t, to], psa.at[t, k], plan["s1"][t] + k, to, me)

        loop(1, ndp, send)

    def sum_middle(t):
        loop(1, ndp, lambda k: arrived(psa.at[t, k], plan["s1"][t] + k))
        total = ps1[t, dp]
        for k in range(1, ndp):
            total = total + psa[t, k]
        psb[t] = total
        loop(1, npr, lambda k: started(psb.at[t], psbr.at[t, k], plan["s2"][t] + k, dp, ring(me + k, npr)))

    def sum_last(t):
        loop(1, npr, lambda k: arrived(psbr.at[t, k], plan["s2"][t] + k))
        total = psb[t]
        for k in range(1, npr):
            total = total + psbr[t, k]
        psc[t, dp] = total
        loop(1, ndp, lambda k: started(psc.at[t, dp], psc.at[t, dp], plan["s3"][t] + k, ring(dp + k, ndp), me))

    def sum_wait(t):
        loop(1, ndp, lambda k: arrived(psc.at[t, ring(dp - k, ndp)], plan["s3"][t] + k))

    def sum_drain(t):
        loop(1, ndp, lambda k: gone(ps1.at[t, ring(dp + k, ndp)], plan["s1"][t] + k))
        loop(1, npr, lambda k: gone(psb.at[t], plan["s2"][t] + k))
        loop(1, ndp, lambda k: gone(psc.at[t, dp], plan["s3"][t] + k))

    def spread(t, at, fn, slot):
        for j in range(tiles):
            v = fn(psc[t, j // q, at + j % q : at + j % q + 1, :])
            wb[pl.ds(8 * slot, 8), j * 128 : (j + 1) * 128] = jnp.broadcast_to(v, (8, 128))

    ps1[...] = jnp.zeros_like(ps1)
    ptr[...] = protos[...].astype(F32).T.astype(BF16)
    tokens_start(0)
    tokens_forward(0)
    tokens_wait(0)
    head(0)
    raw_send(0)
    raw_finish(0)
    ag_first(0)
    ag_second(0)
    tokens_start(1)
    ag_third(0)
    ag_wait(0)
    teacher_scores()
    tokens_forward(1)
    row_pass(False)
    put_rows(0, 0)
    sum_send(0)
    tokens_wait(1)
    head(1)
    raw_send(1)
    sum_middle(0)
    raw_finish(1)
    ag_first(1)
    sum_last(0)
    ag_second(1)
    sum_wait(0)
    spread(0, 0, lambda v: 1.0 / (crops * v), 0)
    row_pass(True)
    put_rows(1, 0)
    sum_send(1)
    ag_third(1)
    sum_middle(1)
    ag_wait(1)
    sum_last(1)
    student_scores()
    put_rows(2, 4)
    sum_wait(1)
    spread(1, 0, lambda v: 1.0 / (crops * v), 0)
    row_pass(True)
    put_rows(2, 0)
    sum_send(2)
    sum_middle(2)
    sum_last(2)
    sum_wait(2)
    spread(2, 0, lambda v: 1.0 / v, 0)
    spread(2, 4, lambda v: jnp.log(v) * LOG2E, 1)

    gp_out[...] = jnp.zeros_like(gp_out)
    losst[...] = jnp.zeros_like(losst)
    share = 1.0 / (crops * STUDENT_TEMP)

    def group_grads(zz, cc):
        lane0 = pl.multiple_of((zz * 2 + cc) * group, group)
        u = units[1, zz, cc]

        def step(b):
            base = pl.multiple_of(b * pb, pb)
            r = pl.ds(base, pb)
            lossa = jnp.zeros((8, 128), F32)
            for j in range(gtiles):
                lanes = pl.ds(pl.multiple_of(lane0 + j * 128, 128), 128)
                inv, norm = wb[0:8, lanes], wb[8:16, lanes]
                for a in range(0, pb, 16):
                    outs = []
                    for h in (0, 8):
                        rr = pl.ds(base + a + h, 8)
                        tgt = ex[rr, lanes] * colb[rr, :] * inv
                        rel = lg2[rr, lanes] - norm
                        lossa = lossa - tgt * rel
                        outs.append((jnp.exp2(rel) - tgt) * share)
                    gt[pl.ds(base + a, 16), j * 128 : (j + 1) * 128] = jnp.concatenate(outs, axis=0).astype(BF16)
            losst[...] += lossa
            gp_out[r, :] += jnp.dot(gt[r, :], u, preferred_element_type=F32)

        loop(0, kp // pb, step)
        ugt[...] = jnp.dot(ptr[...], gt[...], preferred_element_type=F32)
        return ugt[...].T

    for k in range(nz):
        zz = ring(z + 1 + k, nz)
        sibs[k] = group_grads(zz, 1 - c)
        started(sibs.at[k], sibr.at[k], plan["g0"] + k, sib, me)
    for k in range(nz):
        zz = ring(z + 1 + k, nz)
        mine = group_grads(zz, c)
        arrived(sibr.at[k], plan["g0"] + k)
        part[zz] = mine + sibr[k]
        if k < nz - 1:
            started(part.at[zz, :, lo], zrecv.at[k], plan["gz"] + k, zz * 2 + c, me)

        def send(m, zz=zz):
            to = ring(me + m, npr)
            started(part.at[zz, rows(to), hi], precv.at[m, zz], plan["gp"] + m, dp, to)

        loop(1, npr, send)

    losst[...] = losst[...] * (LN2 / crops)
    loop(1, npr, lambda k: started(losst, lossr.at[k], plan["l1"] + k, dp, ring(me + k, npr)))

    total = part[z, :, lo]
    for k in range(nz - 1):
        arrived(zrecv.at[k], plan["gz"] + k)
        total = total + zrecv[k]
    a2[...] = total
    loop(1, npr, lambda k: started(a2.at[rows(ring(me + k, npr))], a2r.at[k], plan["ga"] + k, dp, ring(me + k, npr)))

    loop(1, npr, lambda k: arrived(precv.at[k], plan["gp"] + k))
    b2[...] = lax.fori_loop(1, npr, lambda k, s: s + precv[k], part[:, rows(me), hi])
    for k in range(1, nz):
        zz = ring(z + k, nz)
        started(b2.at[zz], b2r.at[k], plan["gb"] + k, zz * 2 + c, me)

    loop(1, npr, lambda k: arrived(lossr.at[k], plan["l1"] + k))
    lossd[...] = lax.fori_loop(1, npr, lambda k, s: s + lossr[k], losst[...])
    loop(1, ndp, lambda k: started(lossd, lossdr.at[k], plan["l2"] + k, ring(dp + k, ndp), me))

    loop(1, npr, lambda k: arrived(a2r.at[k], plan["ga"] + k))
    grad_lo = lax.fori_loop(1, npr, lambda k, s: s + a2r[k], a2[rows(me), :])
    grad_hi = b2[z]
    for k in range(1, nz):
        arrived(b2r.at[k], plan["gb"] + k)
        grad_hi = grad_hi + b2r[k]

    unit_grad = jnp.concatenate([grad_lo, grad_hi], axis=1)
    own = own_float[...]
    along = jnp.sum(own * unit_grad, axis=1, keepdims=True)
    rg[rows(me), :] = ((unit_grad - own * along) * own_scale[...]).astype(BF16)
    loop(1, npr, lambda k: started(rg.at[rows(me)], rg.at[rows(me)], plan["r1"] + k, dp, ring(me + k, npr)))
    loop(1, npr, lambda k: arrived(rg.at[rows(ring(me - k, npr))], plan["r1"] + k))

    raw_grad = rg[...]
    pre_grad = (nt_dot(raw_grad, w2s[...]) * gelu_slope(pre_s[...])).astype(BF16)
    w2g = tn_dot(hid_s[...], raw_grad)
    gw[pl.ds(width, hb), :] = w2g[:, :hb]
    gw[pl.ds(width + hb, hb), :] = w2g[:, hb:]
    wchunk = min(width, 256)
    for i in range(width // wchunk):
        sl = slice(i * wchunk, (i + 1) * wchunk)
        gw[sl, :] = tn_dot(tok[1, :, sl], pre_grad)

    whole = gw.shape[0]
    halfw, piece = whole // 2, whole // ndp

    def half_of(cc):
        return pl.ds(pl.multiple_of(cc * halfw, 8), halfw)

    def piece_of(zz):
        return pl.ds(pl.multiple_of(c * halfw + zz * piece, 8), piece)

    started(gw.at[half_of(1 - c)], gwr, plan["w0"], sib, me)
    arrived(gwr, plan["w0"])
    gw[half_of(c), :] += gwr[...]
    for k in range(1, nz):
        zz = ring(z + k, nz)
        started(gw.at[piece_of(zz)], gwz.at[k], plan["w1"] + k, zz * 2 + c, me)
    total = gw[piece_of(z), :]
    for k in range(1, nz):
        arrived(gwz.at[k], plan["w1"] + k)
        total = total + gwz[k]
    fw[piece_of(z), :] = total
    for k in range(1, nz):
        started(fw.at[piece_of(z)], fw.at[piece_of(z)], plan["w2"] + k, ring(z + k, nz) * 2 + c, me)
    for k in range(1, nz):
        arrived(fw.at[piece_of(ring(z - k, nz))], plan["w2"] + k)
    started(fw.at[half_of(c)], fw.at[half_of(c)], plan["w3"], sib, me)

    loop(1, ndp, lambda k: arrived(lossdr.at[k], plan["l2"] + k))
    loss = lax.fori_loop(1, ndp, lambda k, s: s + lossdr[k], lossd[...])
    loss_out[...] = jnp.sum(jnp.sum(loss, axis=0, keepdims=True), axis=1, keepdims=True)

    arrived(fw.at[half_of(1 - c)], plan["w3"])
    gw1_out[...] = fw[:width, :]
    gw2_out[:, :hb] = fw[width : width + hb, :]
    gw2_out[:, hb:] = fw[width + hb :, :]

    for v in (0, 1):
        tokens_drain(v)
        raw_drain(v)
        ag_drain(v)
    for t in range(3):
        sum_drain(t)
    for k in range(nz):
        gone(sibs.at[k], plan["g0"] + k)
    for k in range(nz - 1):
        gone(part.at[0, :, lo], plan["gz"] + k)
    loop(1, npr, lambda k: gone(precv.at[k], plan["gp"] + k))
    loop(1, npr, lambda k: gone(losst, plan["l1"] + k))
    loop(1, ndp, lambda k: gone(lossd, plan["l2"] + k))
    loop(1, npr, lambda k: gone(a2r.at[k], plan["ga"] + k))
    for k in range(1, nz):
        gone(b2r.at[k], plan["gb"] + k)
        gone(gwz.at[k], plan["w1"] + k)
        gone(gwz.at[k], plan["w2"] + k)
    loop(1, npr, lambda k: gone(rg.at[rows(me)], plan["r1"] + k))
    gone(gwr, plan["w0"])
    gone(gwr, plan["w3"])


def step(dims, s_in, t_in, w1s, w2s, w1t, w2t, protos):
    nz, nx, ny = dims["nz"], dims["nx"], dims["ny"]
    ndp, npr = 2 * nz, nx * ny
    rb, width = s_in.shape
    hb, cols = w2s.shape
    kp = protos.shape[0]
    group = rb * npr
    crops = group * ndp
    half = cols // 2
    dims = dict(dims, rb=rb, q=group // 128)

    sems = Sems()
    plan = {
        name: [sems.take(n) for _ in range(2)]
        for name, n in dict(
            tx=nx, ty=ny, fa=nx * ny, fb=nx * ny, rr=npr, a1=npr, a2=nz, b1=nz, b2=npr, sa=nz, sb=1
        ).items()
    }
    for name, n in dict(s1=ndp, s2=npr, s3=ndp).items():
        plan[name] = [sems.take(n) for _ in range(3)]
    for name, n in dict(
        g0=nz, gz=nz, gp=npr, ga=npr, gb=nz, l1=npr, l2=ndp, r1=npr, w0=1, w1=nz, w2=nz, w3=1
    ).items():
        plan[name] = sems.take(n)

    wrows = width + 2 * hb
    V = pltpu.VMEM
    scratch = [
        V((2, group, width), BF16),
        V((group, hb), F32),
        V((group, hb), BF16),
        V((2, group, cols), F32),
        V((2, npr, rb, cols), F32),
        V((2, nz, 2, group, cols), BF16),
        V((rb, cols), F32),
        V((rb, 1), F32),
        V((kp, crops), F32),
        V((kp, crops), F32),
        V((kp, 128), F32),
        V((16, crops), F32),
        V((8, crops), F32),
        V((3, ndp, 8, 128), F32),
        V((3, ndp, 8, 128), F32),
        V((3, 8, 128), F32),
        V((3, npr, 8, 128), F32),
        V((3, ndp, 8, 128), F32),
        V((kp, group), BF16),
        V((cols, kp), BF16),
        V((cols, group), F32),
        V((nz, group, cols), F32),
        V((nz, group, cols), F32),
        V((nz, group, cols), F32),
        V((nz - 1, group, half), F32),
        V((npr, nz, rb, half), F32),
        V((group, half), F32),
        V((npr, rb, half), F32),
        V((nz, rb, half), F32),
        V((nz, rb, half), F32),
        V((8, 128), F32),
        V((npr, 8, 128), F32),
        V((8, 128), F32),
        V((ndp, 8, 128), F32),
        V((group, cols), BF16),
        V((wrows, hb), F32),
        V((wrows // 2, hb), F32),
        V((nz, wrows // ndp, hb), F32),
        V((wrows, hb), F32),
        pltpu.SemaphoreType.DMA((sems.count,)),
        pltpu.SemaphoreType.DMA((sems.count,)),
    ]
    vmem = pl.BlockSpec(memory_space=pltpu.VMEM)
    gp, gw1, gw2, loss = pl.pallas_call(
        functools.partial(kernel, dims, plan),
        out_shape=(
            jax.ShapeDtypeStruct((kp, cols), F32),
            jax.ShapeDtypeStruct((width, hb), F32),
            jax.ShapeDtypeStruct((hb, cols), F32),
            jax.ShapeDtypeStruct((1, 1), F32),
        ),
        in_specs=[vmem] * 7,
        out_specs=(vmem,) * 4,
        scratch_shapes=scratch,
        compiler_params=pltpu.CompilerParams(
            collective_id=0, has_side_effects=True, vmem_limit_bytes=63 * 1024 * 1024
        ),
        cost_estimate=pl.CostEstimate(
            flops=8 * kp * crops * cols, bytes_accessed=4 * kp * cols * 4, transcendentals=2 * kp * crops
        ),
    )(s_in, t_in, w1s, w2s, w1t, w2t, protos)
    return gp, gw1, gw2, loss[0, 0]


def solution(mesh):
    ndp, npr = mesh.shape["dp"], mesh.shape["proto"]
    side = math.isqrt(npr)
    dims = dict(nz=ndp // 2, nx=side, ny=npr // side)
    both = P(("dp", "proto"), None)
    return jax.shard_map(
        functools.partial(step, dims),
        mesh=mesh,
        in_specs=(both, both, P(None, "proto"), P("proto", None), P(None, "proto"), P("proto", None), both),
        out_specs=(both, P(None, "proto"), P("proto", None), P()),
        check_vma=False,
    )
```

```python
import functools
import math

import jax
import jax.numpy as jnp
from jax import lax
from jax.experimental import pallas as pl
from jax.experimental.pallas import tpu as pltpu
from jax.sharding import PartitionSpec as P

MESH = pl.DeviceIdType.MESH
TEACHER_TEMP = 0.07
STUDENT_TEMP = 0.1
LOG2E = 1.4426950408889634
LN2 = 0.6931471805599453
F32 = jnp.float32
BF16 = jnp.bfloat16


def normal_cdf(x):
    return 0.5 * (1.0 + lax.erf(x * (1.0 / math.sqrt(2.0))))


def gelu(x):
    return x * normal_cdf(x)


def gelu_slope(x):
    return normal_cdf(x) + x * (jnp.exp(-0.5 * x * x) * (1.0 / math.sqrt(2.0 * math.pi)))


def nt_dot(a, b):
    return lax.dot_general(a, b, (((1,), (1,)), ((), ())), preferred_element_type=F32)


def tn_dot(a, b):
    return lax.dot_general(a, b, (((0,), (0,)), ((), ())), preferred_element_type=F32)


def unit_scale(raw):
    return lax.rsqrt(jnp.sum(raw * raw, axis=1, keepdims=True) + 1e-06)


def kernel(dims, plan, s_in, t_in, w1s_in, w2s_in, w1t_in, w2t_in, protos_in, gp_out, gw1_out, gw2_out, loss_out, *scratch):
    nz, nx, ny, rb, q = dims["nz"], dims["nx"], dims["ny"], dims["rb"], dims["q"]
    ndp, npr = 2 * nz, nx * ny
    width, hb, cols, kp = w1s_in.shape[0], w1s_in.shape[1], w2s_in.shape[1], protos_in.shape[0]
    group = rb * npr
    crops = group * ndp
    total_protos = kp * ndp * npr
    tiles = crops // 128
    part_rows = max(8, tiles)
    half = cols // 2
    (w1s, w2s, w1t, w2t, protos, tok, pre_s, hid_s, rawp, rawr, units, own_float, own_scale, ex, lg2, colb, wb, rows8,
     ps1, psa, psb, psbr, psc, gt, ptr, ugt, sibs, sibr, part, zrecv, precv, a2, a2r, b2, b2r, losst, lossr, lossd,
     lossdr, rg, gw, gwr, gwz, fw, ssem, rsem, lsem) = scratch

    dp, me = lax.axis_index("dp"), lax.axis_index("proto")
    z, c = dp // 2, dp % 2
    x, y = me // ny, me % ny

    def started(src, dst, name, to_dp, to_proto, nth=0):
        s, r = plan[name]
        pltpu.make_async_remote_copy(
            src_ref=src, dst_ref=dst, send_sem=ssem.at[s], recv_sem=rsem.at[r + nth],
            device_id=(to_dp, to_proto), device_id_type=MESH,
        ).start()

    def arrived(dst, name, nth=0):
        pltpu.make_async_copy(dst, dst, rsem.at[plan[name][1] + nth]).wait()

    def gone(src, name):
        pltpu.make_async_copy(src, src, ssem.at[plan[name][0]]).wait()

    def loop(lo, hi, fn, unroll=1):
        def step(k, carry):
            fn(k)
            return carry

        lax.fori_loop(lo, hi, step, 0, unroll=unroll)

    def proto_of(xx, yy):
        return lax.rem(xx + nx, nx) * ny + lax.rem(yy + ny, ny)

    def rows(p):
        return pl.ds(pl.multiple_of(p * rb, rb), rb)

    def ring(value, n):
        return lax.rem(value + n, n)

    inputs = (t_in, s_in)
    w1_of, w2_of = (w1t, w1s), (w2t, w2s)
    left, right = pl.ds(0, width // 2), pl.ds(width // 2, width // 2)
    lo, hi = pl.ds(0, half), pl.ds(half, half)
    sib = dp + 1 - 2 * c

    loads = [
        pltpu.make_async_copy(src, dst, lsem.at[n])
        for n, (src, dst) in enumerate(
            [(t_in, tok.at[0, rows(me)]), (s_in, tok.at[1, rows(me)]), (w1t_in, w1t), (w2t_in, w2t),
             (protos_in, protos), (w1s_in, w1s), (w2s_in, w2s)]
        )
    ]
    for load in loads:
        load.start()

    barrier = pltpu.get_barrier_semaphore()

    def greet_proto(k):
        pl.semaphore_signal(barrier, inc=1, device_id=(dp, ring(me + k, npr)), device_id_type=MESH)

    def greet_dp(k):
        pl.semaphore_signal(barrier, inc=1, device_id=(ring(dp + k, ndp), me), device_id_type=MESH)

    loop(1, npr, greet_proto)
    loop(1, ndp, greet_dp)
    loads[0].wait()
    loads[1].wait()
    pl.semaphore_wait(barrier, npr - 1 + ndp - 1)

    def tokens_start(v):
        mine = tok.at[v, rows(me)]
        for k in range(1, nx):
            started(mine, mine, f"tx{v}", dp, proto_of(x + k, y), k)
        for k in range(1, ny):
            started(mine, mine, f"ty{v}", dp, proto_of(x, y + k), k)

    def tokens_forward(v):
        for k in range(1, max(nx, ny)):
            if k < nx:
                block = rows(proto_of(x - k, y))
                arrived(tok.at[v, block], f"tx{v}", k)
                ref = tok.at[v, block, left]
                for m in range(1, ny):
                    started(ref, ref, f"fa{v}", dp, proto_of(x, y + m))
            if k < ny:
                block = rows(proto_of(x, y - k))
                arrived(tok.at[v, block], f"ty{v}", k)
                ref = tok.at[v, block, right]
                for m in range(1, nx):
                    started(ref, ref, f"fb{v}", dp, proto_of(x + m, y))

    diagonal = pl.ds(0, (nx - 1) * (ny - 1) * rb)

    def tokens_wait(v):
        arrived(tok.at[v, diagonal, left], f"fa{v}")
        arrived(tok.at[v, diagonal, right], f"fb{v}")

    def tokens_drain(v):
        gone(tok.at[v, pl.ds(0, (nx - 1) * rb)], f"tx{v}")
        gone(tok.at[v, pl.ds(0, (ny - 1) * rb)], f"ty{v}")
        gone(tok.at[v, diagonal, left], f"fa{v}")
        gone(tok.at[v, diagonal, right], f"fb{v}")

    def head(v):
        step = min(group, 256)

        def chunk(i):
            r = pl.ds(pl.multiple_of(i * step, step), step)
            pre = jnp.dot(tok[v, r, :], w1_of[v][...], preferred_element_type=F32)
            hidden = gelu(pre).astype(BF16)
            if v == 1:
                pre_s[r, :] = pre
                hid_s[r, :] = hidden
            rawp[v, r, :] = jnp.dot(hidden, w2_of[v][...], preferred_element_type=F32)

        loop(0, group // step, chunk, unroll=group // step)

    def raw_send(v):
        def send(k):
            to = ring(me + k, npr)
            started(rawp.at[v, rows(to)], rawr.at[v, k], f"rr{v}", dp, to)

        loop(1, npr, send)

    others = pl.ds(1, npr - 1)

    def raw_finish(v):
        arrived(rawr.at[v, others], f"rr{v}")
        raw = rawp[v, rows(me), :]
        for k in range(1, npr):
            raw = raw + rawr[v, k]
        scale = unit_scale(raw)
        unit_float = raw * scale
        if v == 1:
            own_float[...] = unit_float
            own_scale[...] = scale
        units[v, z, c, rows(me), :] = unit_float.astype(BF16)

    def raw_drain(v):
        gone(rawr.at[v, others], f"rr{v}")

    def band(xx):
        return pl.ds(pl.multiple_of(ring(xx, nx) * (ny * rb), ny * rb), ny * rb)

    def ag_first(v):
        mine = units.at[v, z, c, rows(me)]
        for k in range(1, nz):
            started(mine.at[:, hi], mine.at[:, hi], f"b1{v}", ring(z + k, nz) * 2 + c, me)
        loop(1, npr, lambda k: started(mine.at[:, lo], mine.at[:, lo], f"a1{v}", dp, ring(me + k, npr)))

    def ag_second(v):
        arrived(units.at[v, pl.ds(0, nz - 1), c, rows(me), hi], f"b1{v}")
        col = units.at[v, :, c, rows(me), hi]
        for kx in range(nx):
            for ky in range(ny):
                if kx or ky:
                    started(col, col, f"b2{v}", dp, proto_of(x + kx, y + ky), kx)
        arrived(units.at[v, z, c, pl.ds(0, (npr - 1) * rb), lo], f"a1{v}")
        plane = units.at[v, z, c, :, lo]
        for k in range(1, nz):
            started(plane, plane, f"a2{v}", ring(z + k, nz) * 2 + c, me, k)
        started(plane, plane, f"sa{v}", sib, me)

    def ag_third(v):
        for k in range(1, nz):
            plane = units.at[v, ring(z - k, nz), c, :, lo]
            arrived(plane, f"a2{v}", k)
            started(plane, plane, f"sa{v}", sib, me)
        for k in range(nx):
            piece = units.at[v, :, c, band(x - k), hi]
            if k:
                arrived(piece, f"b2{v}", k)
            else:
                arrived(units.at[v, :, c, pl.ds(0, (ny - 1) * rb), hi], f"b2{v}", k)
            started(piece, piece, f"sb{v}", sib, me)

    def ag_wait(v):
        arrived(units.at[v, :, 1 - c, :, lo], f"sa{v}")
        arrived(units.at[v, :, 1 - c, :, hi], f"sb{v}")

    def ag_drain(v):
        gone(units.at[v, z, c, pl.ds(0, (npr - 1) * rb), lo], f"a1{v}")
        gone(units.at[v, pl.ds(0, nz - 1), c, rows(me), hi], f"b1{v}")
        gone(units.at[v, :, c, pl.ds(0, (npr - 1) * rb), hi], f"b2{v}")
        gone(units.at[v, pl.ds(0, nz - 1), c, :, lo], f"a2{v}")
        gone(units.at[v, :, c, :, lo], f"sa{v}")
        gone(units.at[v, :, c, :, hi], f"sb{v}")

    pb = min(kp, 256)
    nb = kp // pb
    gtiles = group // 128

    def teacher_scores(cc):
        def step(i):
            zz, b = i // nb, i % nb
            r = pl.ds(pl.multiple_of(b * pb, pb), pb)
            s = nt_dot(protos[r, :], units[0, zz, cc])
            e = jnp.exp2(s * (LOG2E / TEACHER_TEMP))
            ex[r, pl.ds(pl.multiple_of((2 * zz + cc) * group, group), group)] = e
            acc = e[:, :128]
            for j in range(1, gtiles):
                acc = acc + e[:, j * 128 : (j + 1) * 128]
            colb[r, :] += acc

        loop(0, nz * nb, step, unroll=2 * nb)

    def first_scales():
        def scale(i):
            r = pl.ds(pl.multiple_of(i * 64, 64), 64)
            total = jnp.sum(colb[r, :], axis=1, keepdims=True)
            colb[r, :] = jnp.broadcast_to(1.0 / (total_protos * total), (64, 128))

        loop(0, kp // 64, scale, unroll=2)

    def student_scores(cc):
        def step(i):
            zz, b = i // nb, i % nb
            r = pl.ds(pl.multiple_of(b * pb, pb), pb)
            lanes = pl.ds(pl.multiple_of((2 * zz + cc) * group, group), group)
            s = nt_dot(protos[r, :], units[1, zz, cc]) * (LOG2E / STUDENT_TEMP)
            lg2[r, lanes] = s
            rows8[:, lanes] += jnp.sum(jnp.exp2(s).reshape(pb // 8, 8, group), axis=0)

        loop(0, nz * nb, step, unroll=2 * nb)

    def row_pass(fresh):
        rows8[...] = jnp.zeros_like(rows8)

        def step(i):
            base = pl.multiple_of(i * 64, 64)
            if fresh:
                accs = [None] * 8
                for j in range(tiles):
                    lanes = slice(j * 128, (j + 1) * 128)
                    w = wb[0:8, lanes]
                    for a in range(8):
                        term = ex[pl.ds(base + 8 * a, 8), lanes] * w
                        accs[a] = term if accs[a] is None else accs[a] + term
                scales = []
                for a in range(8):
                    total = jnp.sum(accs[a], axis=1, keepdims=True)
                    scale = jnp.broadcast_to(1.0 / (total_protos * total), (8, 128))
                    colb[pl.ds(base + 8 * a, 8), :] = scale
                    scales.append(scale)
            else:
                scales = [colb[pl.ds(base + 8 * a, 8), :] for a in range(8)]
            for j in range(tiles):
                lanes = slice(j * 128, (j + 1) * 128)
                terms = [ex[pl.ds(base + 8 * a, 8), lanes] * scales[a] for a in range(8)]
                while len(terms) > 1:
                    terms = [terms[n] + terms[n + 1] for n in range(0, len(terms), 2)]
                rows8[:, lanes] += terms[0]

        loop(0, kp // 64, step, unroll=2)

    def put_rows(t, at):
        for j in range(tiles):
            ps1[t, at * part_rows + j : at * part_rows + j + 1, :] = jnp.sum(
                rows8[:, j * 128 : (j + 1) * 128], axis=0, keepdims=True
            )

    def span(t):
        return pl.ds(0, part_rows * (2 if t == 2 else 1))

    def sum_send(t):
        for k in range(1, ndp):
            started(ps1.at[t, span(t)], psa.at[t, k, span(t)], f"s1{t}", ring(dp + k, ndp), me)

    def sum_middle(t):
        arrived(psa.at[t, pl.ds(1, ndp - 1), span(t)], f"s1{t}")
        total = ps1[t, span(t), :]
        for k in range(1, ndp):
            total = total + psa[t, k, span(t), :]
        psb[t, span(t), :] = total
        for k in range(1, npr):
            started(psb.at[t, span(t)], psbr.at[t, k, span(t)], f"s2{t}", dp, ring(me + k, npr))

    def sum_finish(t):
        arrived(psbr.at[t, others, span(t)], f"s2{t}")
        total = psb[t, span(t), :]
        for k in range(1, npr):
            total = total + psbr[t, k, span(t), :]
        psc[t, span(t), :] = total

    def sum_drain(t):
        gone(psa.at[t, pl.ds(1, ndp - 1), span(t)], f"s1{t}")
        gone(psbr.at[t, others, span(t)], f"s2{t}")

    def spread(t, at, fn, slot):
        for j in range(tiles):
            v = fn(psc[t, at * part_rows + j : at * part_rows + j + 1, :])
            wb[pl.ds(8 * slot, 8), j * 128 : (j + 1) * 128] = jnp.broadcast_to(v, (8, 128))

    def next_weight(v):
        return 1.0 / (crops * v)

    tokens_start(0)
    ps1[...] = jnp.zeros_like(ps1)
    colb[...] = jnp.zeros_like(colb)
    for load in loads[2:]:
        load.wait()
    tokens_forward(0)
    ptr[...] = protos[...].astype(F32).T.astype(BF16)
    tokens_wait(0)
    head(0)
    raw_send(0)
    raw_finish(0)
    ag_first(0)
    tokens_start(1)
    ag_second(0)
    tokens_forward(1)
    ag_third(0)
    teacher_scores(c)
    ag_wait(0)
    teacher_scores(1 - c)
    tokens_wait(1)
    head(1)
    raw_send(1)
    first_scales()
    row_pass(False)
    put_rows(0, 0)
    sum_send(0)
    sum_middle(0)
    raw_finish(1)
    ag_first(1)
    sum_finish(0)
    spread(0, 0, next_weight, 0)
    row_pass(True)
    put_rows(1, 0)
    sum_send(1)
    ag_second(1)
    sum_middle(1)
    ag_third(1)
    rows8[...] = jnp.zeros_like(rows8)
    student_scores(c)
    ag_wait(1)
    student_scores(1 - c)
    put_rows(2, 1)
    sum_finish(1)
    spread(1, 0, next_weight, 0)
    row_pass(True)
    put_rows(2, 0)
    sum_send(2)
    sum_middle(2)
    sum_finish(2)
    spread(2, 0, lambda v: 1.0 / v, 0)
    spread(2, 1, lambda v: jnp.log(v) * LOG2E, 1)

    gp_out[...] = jnp.zeros_like(gp_out)
    losst[...] = jnp.zeros_like(losst)
    share = 1.0 / (crops * STUDENT_TEMP)

    def group_grads(zz, cc):
        lane0 = pl.multiple_of((zz * 2 + cc) * group, group)
        u = units[1, zz, cc]

        def step(b):
            base = pl.multiple_of(b * pb, pb)
            r = pl.ds(base, pb)
            lossa = jnp.zeros((8, 128), F32)
            for j in range(gtiles):
                lanes = pl.ds(pl.multiple_of(lane0 + j * 128, 128), 128)
                inv, norm = wb[0:8, lanes], wb[8:16, lanes]
                for a in range(0, pb, 16):
                    outs = []
                    for h in (0, 8):
                        rr = pl.ds(base + a + h, 8)
                        tgt = ex[rr, lanes] * colb[rr, :] * inv
                        rel = lg2[rr, lanes] - norm
                        lossa = lossa - tgt * rel
                        outs.append((jnp.exp2(rel) - tgt) * share)
                    gt[pl.ds(base + a, 16), j * 128 : (j + 1) * 128] = jnp.concatenate(outs, axis=0).astype(BF16)
            losst[...] += lossa
            gp_out[r, :] += jnp.dot(gt[r, :], u, preferred_element_type=F32)

        loop(0, nb, step, unroll=nb)
        ugt[...] = jnp.dot(ptr[...], gt[...], preferred_element_type=F32)
        return ugt[...].T

    for k in range(nz):
        zz = ring(z + 1 + k, nz)
        sibs[k] = group_grads(zz, 1 - c)
        started(sibs.at[k], sibr.at[k], "g0", sib, me, k)
        mine = group_grads(zz, c)
        arrived(sibr.at[k], "g0", k)
        part[zz] = mine + sibr[k]
        if k < nz - 1:
            started(part.at[zz, :, lo], zrecv.at[k], "gz", zz * 2 + c, me)

        def send(m, zz=zz):
            to = ring(me + m, npr)
            started(part.at[zz, rows(to), hi], precv.at[m, zz], "gp", dp, to)

        loop(1, npr, send)

    arrived(zrecv, "gz")
    total = part[z, :, lo]
    for k in range(nz - 1):
        total = total + zrecv[k]
    a2[...] = total
    loop(1, npr, lambda k: started(a2.at[rows(ring(me + k, npr))], a2r.at[k], "ga", dp, ring(me + k, npr)))

    arrived(precv.at[others], "gp")
    total = part[:, rows(me), hi]
    for k in range(1, npr):
        total = total + precv[k]
    b2[...] = total
    for k in range(1, nz):
        zz = ring(z + k, nz)
        started(b2.at[zz], b2r.at[k], "gb", zz * 2 + c, me)

    losst[...] = losst[...] * (LN2 / crops)
    loop(1, npr, lambda k: started(losst, lossr.at[k], "l1", dp, ring(me + k, npr)))

    arrived(b2r.at[pl.ds(1, nz - 1)], "gb")
    grad_hi = b2[z]
    for k in range(1, nz):
        grad_hi = grad_hi + b2r[k]
    arrived(a2r.at[others], "ga")
    grad_lo = a2[rows(me), :]
    for k in range(1, npr):
        grad_lo = grad_lo + a2r[k]

    unit_grad = jnp.concatenate([grad_lo, grad_hi], axis=1)
    own = own_float[...]
    along = jnp.sum(own * unit_grad, axis=1, keepdims=True)
    rg[rows(me), :] = ((unit_grad - own * along) * own_scale[...]).astype(BF16)
    loop(1, npr, lambda k: started(rg.at[rows(me)], rg.at[rows(me)], "r1", dp, ring(me + k, npr)))

    arrived(lossr.at[others], "l1")
    total = losst[...]
    for k in range(1, npr):
        total = total + lossr[k]
    lossd[...] = total
    loop(1, ndp, lambda k: started(lossd, lossdr.at[k], "l2", ring(dp + k, ndp), me))
    pre_s[...] = gelu_slope(pre_s[...])

    arrived(rg.at[pl.ds(0, (npr - 1) * rb)], "r1")
    raw_grad = rg[...]
    pre_grad = (nt_dot(raw_grad, w2s[...]) * pre_s[...]).astype(BF16)
    w2g = tn_dot(hid_s[...], raw_grad)
    gw[pl.ds(width, hb), :] = w2g[:, :hb]
    gw[pl.ds(width + hb, hb), :] = w2g[:, hb:]
    wchunk = min(width, 256)
    for i in range(width // wchunk):
        sl = slice(i * wchunk, (i + 1) * wchunk)
        gw[sl, :] = tn_dot(tok[1, :, sl], pre_grad)

    whole = gw.shape[0]
    halfw, piece = whole // 2, whole // ndp

    def half_of(cc):
        return pl.ds(pl.multiple_of(cc * halfw, 8), halfw)

    def piece_of(zz):
        return pl.ds(pl.multiple_of(c * halfw + zz * piece, 8), piece)

    started(gw.at[half_of(1 - c)], gwr, "w0", sib, me)
    arrived(gwr, "w0")
    gw[half_of(c), :] += gwr[...]
    for k in range(1, nz):
        zz = ring(z + k, nz)
        started(gw.at[piece_of(zz)], gwz.at[k], "w1", zz * 2 + c, me)
    total = gw[piece_of(z), :]
    arrived(gwz.at[pl.ds(1, nz - 1)], "w1")
    for k in range(1, nz):
        total = total + gwz[k]
    fw[piece_of(z), :] = total
    for k in range(1, nz):
        started(fw.at[piece_of(z)], fw.at[piece_of(z)], "w2", ring(z + k, nz) * 2 + c, me)
    arrived(gwz.at[pl.ds(1, nz - 1)], "w2")
    started(fw.at[half_of(c)], fw.at[half_of(c)], "w3", sib, me)

    arrived(lossdr.at[pl.ds(1, ndp - 1)], "l2")
    loss = lossd[...]
    for k in range(1, ndp):
        loss = loss + lossdr[k]
    loss_out[...] = jnp.sum(jnp.sum(loss, axis=0, keepdims=True), axis=1, keepdims=True)

    for v in (0, 1):
        tokens_drain(v)
        raw_drain(v)
        ag_drain(v)
    for t in range(3):
        sum_drain(t)
    gone(sibs, "g0")
    gone(zrecv, "gz")
    gone(precv.at[others], "gp")
    gone(a2r.at[others], "ga")
    gone(b2r.at[pl.ds(1, nz - 1)], "gb")
    gone(lossr.at[others], "l1")
    gone(lossdr.at[pl.ds(1, ndp - 1)], "l2")
    gone(rg.at[pl.ds(0, (npr - 1) * rb)], "r1")
    gone(gwr, "w0")
    gone(gwz.at[pl.ds(1, nz - 1)], "w1")
    gone(gwz.at[pl.ds(1, nz - 1)], "w2")

    arrived(fw.at[half_of(1 - c)], "w3")
    gw1_out[...] = fw[:width, :]
    gw2_out[:, :hb] = fw[width : width + hb, :]
    gw2_out[:, hb:] = fw[width + hb :, :]
    gone(gwr, "w3")


def step(dims, s_in, t_in, w1s, w2s, w1t, w2t, protos):
    nz, nx, ny = dims["nz"], dims["nx"], dims["ny"]
    ndp, npr = 2 * nz, nx * ny
    rb, width = s_in.shape
    hb, cols = w2s.shape
    kp = protos.shape[0]
    group = rb * npr
    crops = group * ndp
    half = cols // 2
    dims = dict(dims, rb=rb, q=group // 128)

    plan, n_send, n_recv = {}, 0, 0
    phases = [(f"{name}{v}", n) for v in (0, 1) for name, n in dict(
        tx=nx, ty=ny, fa=1, fb=1, rr=1, a1=1, b1=1, b2=nx, a2=nz, sa=1, sb=1).items()]
    phases += [(f"{name}{t}", 1) for t in range(3) for name in ("s1", "s2")]
    phases += [("g0", nz)] + [(n, 1) for n in ("gz", "gp", "ga", "gb", "l1", "l2", "r1", "w0", "w1", "w2", "w3")]
    for name, n in phases:
        plan[name] = (n_send, n_recv)
        n_send, n_recv = n_send + 1, n_recv + n
    part_rows = max(8, crops // 128)

    wrows = width + 2 * hb
    V = pltpu.VMEM
    scratch = [
        V((width, hb), BF16),
        V((hb, cols), BF16),
        V((width, hb), BF16),
        V((hb, cols), BF16),
        V((kp, cols), BF16),
        V((2, group, width), BF16),
        V((group, hb), F32),
        V((group, hb), BF16),
        V((2, group, cols), F32),
        V((2, npr, rb, cols), F32),
        V((2, nz, 2, group, cols), BF16),
        V((rb, cols), F32),
        V((rb, 1), F32),
        V((kp, crops), F32),
        V((kp, crops), F32),
        V((kp, 128), F32),
        V((16, crops), F32),
        V((8, crops), F32),
        V((3, 2 * part_rows, 128), F32),
        V((3, ndp, 2 * part_rows, 128), F32),
        V((3, 2 * part_rows, 128), F32),
        V((3, npr, 2 * part_rows, 128), F32),
        V((3, 2 * part_rows, 128), F32),
        V((kp, group), BF16),
        V((cols, kp), BF16),
        V((cols, group), F32),
        V((nz, group, cols), F32),
        V((nz, group, cols), F32),
        V((nz, group, cols), F32),
        V((nz - 1, group, half), F32),
        V((npr, nz, rb, half), F32),
        V((group, half), F32),
        V((npr, rb, half), F32),
        V((nz, rb, half), F32),
        V((nz, rb, half), F32),
        V((8, 128), F32),
        V((npr, 8, 128), F32),
        V((8, 128), F32),
        V((ndp, 8, 128), F32),
        V((group, cols), BF16),
        V((wrows, hb), F32),
        V((wrows // 2, hb), F32),
        V((nz, wrows // ndp, hb), F32),
        V((wrows, hb), F32),
        pltpu.SemaphoreType.DMA((n_send,)),
        pltpu.SemaphoreType.DMA((n_recv,)),
        pltpu.SemaphoreType.DMA((7,)),
    ]
    vmem = pl.BlockSpec(memory_space=pltpu.VMEM)
    gp, gw1, gw2, loss = pl.pallas_call(
        functools.partial(kernel, dims, plan),
        out_shape=(
            jax.ShapeDtypeStruct((kp, cols), F32),
            jax.ShapeDtypeStruct((width, hb), F32),
            jax.ShapeDtypeStruct((hb, cols), F32),
            jax.ShapeDtypeStruct((1, 1), F32),
        ),
        in_specs=[pl.BlockSpec(memory_space=pl.ANY)] * 7,
        out_specs=(vmem,) * 4,
        scratch_shapes=scratch,
        compiler_params=pltpu.CompilerParams(
            collective_id=0, has_side_effects=True, vmem_limit_bytes=63 * 1024 * 1024
        ),
        cost_estimate=pl.CostEstimate(
            flops=8 * kp * crops * cols, bytes_accessed=4 * kp * cols * 4, transcendentals=2 * kp * crops
        ),
    )(s_in, t_in, w1s, w2s, w1t, w2t, protos)
    return gp, gw1, gw2, loss[0, 0]


def solution(mesh):
    ndp, npr = mesh.shape["dp"], mesh.shape["proto"]
    side = math.isqrt(npr)
    dims = dict(nz=ndp // 2, nx=side, ny=npr // side)
    both = P(("dp", "proto"), None)
    return jax.shard_map(
        functools.partial(step, dims),
        mesh=mesh,
        in_specs=(both, both, P(None, "proto"), P("proto", None), P(None, "proto"), P("proto", None), both),
        out_specs=(both, P(None, "proto"), P("proto", None), P()),
        check_vma=False,
    )
```

```python
import functools
import math

import jax
import jax.numpy as jnp
from jax import lax
from jax.experimental import pallas as pl
from jax.experimental.pallas import tpu as pltpu
from jax.sharding import PartitionSpec as P

MESH = pl.DeviceIdType.MESH
TEACHER_TEMP = 0.07
STUDENT_TEMP = 0.1
LOG2E = 1.4426950408889634
LN2 = 0.6931471805599453
F32 = jnp.float32
BF16 = jnp.bfloat16


def normal_cdf(x):
    return 0.5 * (1.0 + lax.erf(x * (1.0 / math.sqrt(2.0))))


def gelu(x):
    return x * normal_cdf(x)


def gelu_slope(x):
    return normal_cdf(x) + x * (jnp.exp(-0.5 * x * x) * (1.0 / math.sqrt(2.0 * math.pi)))


def nt_dot(a, b):
    return lax.dot_general(a, b, (((1,), (1,)), ((), ())), preferred_element_type=F32)


def tn_dot(a, b):
    return lax.dot_general(a, b, (((0,), (0,)), ((), ())), preferred_element_type=F32)


def unit_scale(raw):
    return lax.rsqrt(jnp.sum(raw * raw, axis=1, keepdims=True) + 1e-06)


def kernel(dims, plan, s_in, t_in, w1s_in, w2s_in, w1t_in, w2t_in, protos_in, gp_out, gw1_out, gw2_out, loss_out, *scratch):
    nz, nx, ny, rb, q = dims["nz"], dims["nx"], dims["ny"], dims["rb"], dims["q"]
    ndp, npr = 2 * nz, nx * ny
    width, hb, cols, kp = w1s_in.shape[0], w1s_in.shape[1], w2s_in.shape[1], protos_in.shape[0]
    group = rb * npr
    crops = group * ndp
    total_protos = kp * ndp * npr
    tiles = crops // 128
    part_rows = max(8, tiles)
    half = cols // 2
    hr = rb // 2
    (w1s, w2s, w1t, w2t, protos, tok, pre_s, hid_s, rawp, rawr, units, own_float, own_scale, ex, lg2, colb, wb, rows8,
     ps1, psa, psb, psbr, psc, gt, ptr, ugt, sibs, sibr, part, zrecv, precv, ohr, a2, a2r, b2, b2r, losst, lossr, lossd,
     lossdr, rg, gw, gwr, gwz, fw, ssem, rsem, lsem) = scratch

    dp, me = lax.axis_index("dp"), lax.axis_index("proto")
    z, c = dp // 2, dp % 2
    x, y = me // ny, me % ny

    def started(src, dst, name, to_dp, to_proto, nth=0):
        s, r = plan[name]
        pltpu.make_async_remote_copy(
            src_ref=src, dst_ref=dst, send_sem=ssem.at[s], recv_sem=rsem.at[r + nth],
            device_id=(to_dp, to_proto), device_id_type=MESH,
        ).start()

    def arrived(dst, name, nth=0):
        pltpu.make_async_copy(dst, dst, rsem.at[plan[name][1] + nth]).wait()

    def gone(src, name):
        pltpu.make_async_copy(src, src, ssem.at[plan[name][0]]).wait()

    def loop(lo, hi, fn, unroll=1):
        def step(k, carry):
            fn(k)
            return carry

        lax.fori_loop(lo, hi, step, 0, unroll=unroll)

    def proto_of(xx, yy):
        return lax.rem(xx + nx, nx) * ny + lax.rem(yy + ny, ny)

    def rows(p):
        return pl.ds(pl.multiple_of(p * rb, rb), rb)

    def hrows(p):
        return pl.ds(pl.multiple_of(p * hr, hr), hr)

    def ring(value, n):
        return lax.rem(value + n, n)

    inputs = (t_in, s_in)
    w1_of, w2_of = (w1t, w1s), (w2t, w2s)
    left, right = pl.ds(0, width // 2), pl.ds(width // 2, width // 2)
    lo, hi = pl.ds(0, half), pl.ds(half, half)
    sib = dp + 1 - 2 * c

    loads = [
        pltpu.make_async_copy(src, dst, lsem.at[n])
        for n, (src, dst) in enumerate(
            [(t_in, tok.at[0, rows(me)]), (s_in, tok.at[1, rows(me)]), (w1t_in, w1t), (w2t_in, w2t),
             (protos_in, protos), (w1s_in, w1s), (w2s_in, w2s)]
        )
    ]
    for load in loads:
        load.start()

    barrier = pltpu.get_barrier_semaphore()

    def greet_proto(k):
        pl.semaphore_signal(barrier, inc=1, device_id=(dp, ring(me + k, npr)), device_id_type=MESH)

    def greet_dp(k):
        pl.semaphore_signal(barrier, inc=1, device_id=(ring(dp + k, ndp), me), device_id_type=MESH)

    loop(1, npr, greet_proto)
    loop(1, ndp, greet_dp)
    loads[0].wait()
    loads[1].wait()
    pl.semaphore_wait(barrier, npr - 1 + ndp - 1)

    def tokens_start(v):
        mine = tok.at[v, rows(me)]
        for k in range(1, nx):
            started(mine, mine, f"tx{v}", dp, proto_of(x + k, y), k)
        for k in range(1, ny):
            started(mine, mine, f"ty{v}", dp, proto_of(x, y + k), k)

    def tokens_forward(v):
        for k in range(1, max(nx, ny)):
            if k < nx:
                block = rows(proto_of(x - k, y))
                arrived(tok.at[v, block], f"tx{v}", k)
                ref = tok.at[v, block, left]
                for m in range(1, ny):
                    started(ref, ref, f"fa{v}", dp, proto_of(x, y + m))
            if k < ny:
                block = rows(proto_of(x, y - k))
                arrived(tok.at[v, block], f"ty{v}", k)
                ref = tok.at[v, block, right]
                for m in range(1, nx):
                    started(ref, ref, f"fb{v}", dp, proto_of(x + m, y))

    diagonal = pl.ds(0, (nx - 1) * (ny - 1) * rb)

    def tokens_wait(v):
        arrived(tok.at[v, diagonal, left], f"fa{v}")
        arrived(tok.at[v, diagonal, right], f"fb{v}")

    def tokens_drain(v):
        gone(tok.at[v, pl.ds(0, (nx - 1) * rb)], f"tx{v}")
        gone(tok.at[v, pl.ds(0, (ny - 1) * rb)], f"ty{v}")
        gone(tok.at[v, diagonal, left], f"fa{v}")
        gone(tok.at[v, diagonal, right], f"fb{v}")

    def head(v):
        step = min(group, 256)

        def chunk(i):
            r = pl.ds(pl.multiple_of(i * step, step), step)
            pre = jnp.dot(tok[v, r, :], w1_of[v][...], preferred_element_type=F32)
            hidden = gelu(pre).astype(BF16)
            if v == 1:
                pre_s[r, :] = pre
                hid_s[r, :] = hidden
            rawp[v, r, :] = jnp.dot(hidden, w2_of[v][...], preferred_element_type=F32)

        loop(0, group // step, chunk, unroll=group // step)

    def raw_send(v):
        def send(k):
            to = ring(me + k, npr)
            started(rawp.at[v, rows(to)], rawr.at[v, k], f"rr{v}", dp, to)

        loop(1, npr, send)

    others = pl.ds(1, npr - 1)

    def raw_finish(v):
        arrived(rawr.at[v, others], f"rr{v}")
        raw = rawp[v, rows(me), :]
        for k in range(1, npr):
            raw = raw + rawr[v, k]
        scale = unit_scale(raw)
        unit_float = raw * scale
        if v == 1:
            own_float[...] = unit_float
            own_scale[...] = scale
        units[v, z, c, :, hrows(me), :] = unit_float.astype(BF16).reshape(2, hr, cols)

    def raw_drain(v):
        gone(rawr.at[v, others], f"rr{v}")

    def band(xx):
        return pl.ds(pl.multiple_of(ring(xx, nx) * (ny * hr), ny * hr), ny * hr)

    def ag_first(v):
        mine = units.at[v, z, c, 1, hrows(me)]
        for k in range(1, nz):
            started(mine.at[:, hi], mine.at[:, hi], f"b1{v}", ring(z + k, nz) * 2 + c, me)
        loop(1, npr, lambda k: started(mine.at[:, lo], mine.at[:, lo], f"a1{v}", dp, ring(me + k, npr)))
        direct = units.at[v, z, c, 0, hrows(me)]
        for kz in list(range(1, nz)) + [0]:

            def send(k, kz=kz):
                started(direct, direct, f"d1{v}", ring(z + kz, nz) * 2 + c, ring(me + k, npr), kz)

            loop(0 if kz else 1, npr, send)

    def ag_second(v):
        arrived(units.at[v, pl.ds(0, nz - 1), c, 1, hrows(me), hi], f"b1{v}")
        col = units.at[v, :, c, 1, hrows(me), hi]
        for kx in range(nx):
            for ky in range(ny):
                if kx or ky:
                    started(col, col, f"b2{v}", dp, proto_of(x + kx, y + ky), kx)
        arrived(units.at[v, z, c, 1, pl.ds(0, (npr - 1) * hr), lo], f"a1{v}")
        plane = units.at[v, z, c, 1, :, lo]
        for k in range(1, nz):
            started(plane, plane, f"a2{v}", ring(z + k, nz) * 2 + c, me, k)
        started(plane, plane, f"sa{v}", sib, me)

    def ag_third(v):
        for k in range(nz):
            plane = units.at[v, ring(z - k, nz), c, 0]
            if k:
                arrived(plane, f"d1{v}", k)
            else:
                arrived(units.at[v, z, c, 0, pl.ds(0, (npr - 1) * hr)], f"d1{v}", k)
            started(plane, plane, f"sd{v}", sib, me)
        for k in range(1, nz):
            plane = units.at[v, ring(z - k, nz), c, 1, :, lo]
            arrived(plane, f"a2{v}", k)
            started(plane, plane, f"sa{v}", sib, me)
        for k in range(nx):
            piece = units.at[v, :, c, 1, band(x - k), hi]
            if k:
                arrived(piece, f"b2{v}", k)
            else:
                arrived(units.at[v, :, c, 1, pl.ds(0, (ny - 1) * hr), hi], f"b2{v}", k)
            started(piece, piece, f"sb{v}", sib, me)

    def ag_wait(v):
        arrived(units.at[v, :, 1 - c, 0], f"sd{v}")
        arrived(units.at[v, :, 1 - c, 1, :, lo], f"sa{v}")
        arrived(units.at[v, :, 1 - c, 1, :, hi], f"sb{v}")

    def ag_drain(v):
        gone(protos.at[pl.ds(0, (nz * npr - 1) * hr)], f"d1{v}")
        gone(units.at[v, :, c, 0], f"sd{v}")
        gone(units.at[v, z, c, 1, pl.ds(0, (npr - 1) * hr), lo], f"a1{v}")
        gone(units.at[v, pl.ds(0, nz - 1), c, 1, hrows(me), hi], f"b1{v}")
        gone(units.at[v, :, c, 1, pl.ds(0, (npr - 1) * hr), hi], f"b2{v}")
        gone(units.at[v, pl.ds(0, nz - 1), c, 1, :, lo], f"a2{v}")
        gone(units.at[v, :, c, 1, :, lo], f"sa{v}")
        gone(units.at[v, :, c, 1, :, hi], f"sb{v}")

    pb = min(kp, 256)
    nb = kp // pb
    gtiles = group // 128

    def teacher_scores(cc):
        def step(i):
            zz, b = i // nb, i % nb
            r = pl.ds(pl.multiple_of(b * pb, pb), pb)
            s = nt_dot(protos[r, :], units[0, zz, cc].reshape(group, cols))
            e = jnp.exp2(s * (LOG2E / TEACHER_TEMP))
            ex[r, pl.ds(pl.multiple_of((2 * zz + cc) * group, group), group)] = e
            acc = e[:, :128]
            for j in range(1, gtiles):
                acc = acc + e[:, j * 128 : (j + 1) * 128]
            colb[r, :] += acc

        loop(0, nz * nb, step, unroll=2 * nb)

    def first_scales():
        def scale(i):
            r = pl.ds(pl.multiple_of(i * 64, 64), 64)
            total = jnp.sum(colb[r, :], axis=1, keepdims=True)
            colb[r, :] = jnp.broadcast_to(1.0 / (total_protos * total), (64, 128))

        loop(0, kp // 64, scale, unroll=2)

    def student_scores(cc):
        def step(i):
            zz, b = i // nb, i % nb
            r = pl.ds(pl.multiple_of(b * pb, pb), pb)
            lanes = pl.ds(pl.multiple_of((2 * zz + cc) * group, group), group)
            s = nt_dot(protos[r, :], units[1, zz, cc].reshape(group, cols)) * (LOG2E / STUDENT_TEMP)
            lg2[r, lanes] = s
            rows8[:, lanes] += jnp.sum(jnp.exp2(s).reshape(pb // 8, 8, group), axis=0)

        loop(0, nz * nb, step, unroll=2 * nb)

    def row_pass(fresh):
        rows8[...] = jnp.zeros_like(rows8)

        def step(i):
            base = pl.multiple_of(i * 64, 64)
            if fresh:
                accs = [None] * 8
                for j in range(tiles):
                    lanes = slice(j * 128, (j + 1) * 128)
                    w = wb[0:8, lanes]
                    for a in range(8):
                        term = ex[pl.ds(base + 8 * a, 8), lanes] * w
                        accs[a] = term if accs[a] is None else accs[a] + term
                scales = []
                for a in range(8):
                    total = jnp.sum(accs[a], axis=1, keepdims=True)
                    scale = jnp.broadcast_to(1.0 / (total_protos * total), (8, 128))
                    colb[pl.ds(base + 8 * a, 8), :] = scale
                    scales.append(scale)
            else:
                scales = [colb[pl.ds(base + 8 * a, 8), :] for a in range(8)]
            for j in range(tiles):
                lanes = slice(j * 128, (j + 1) * 128)
                terms = [ex[pl.ds(base + 8 * a, 8), lanes] * scales[a] for a in range(8)]
                while len(terms) > 1:
                    terms = [terms[n] + terms[n + 1] for n in range(0, len(terms), 2)]
                rows8[:, lanes] += terms[0]

        loop(0, kp // 64, step, unroll=2)

    def put_rows(t, at):
        for j in range(tiles):
            ps1[t, at * part_rows + j : at * part_rows + j + 1, :] = jnp.sum(
                rows8[:, j * 128 : (j + 1) * 128], axis=0, keepdims=True
            )

    def span(t):
        return pl.ds(0, part_rows * (2 if t == 2 else 1))

    def sum_send(t):
        for k in range(1, ndp):
            started(ps1.at[t, span(t)], psa.at[t, k, span(t)], f"s1{t}", ring(dp + k, ndp), me)

    def sum_middle(t):
        arrived(psa.at[t, pl.ds(1, ndp - 1), span(t)], f"s1{t}")
        total = ps1[t, span(t), :]
        for k in range(1, ndp):
            total = total + psa[t, k, span(t), :]
        psb[t, span(t), :] = total
        for k in range(1, npr):
            started(psb.at[t, span(t)], psbr.at[t, k, span(t)], f"s2{t}", dp, ring(me + k, npr))

    def sum_finish(t):
        arrived(psbr.at[t, others, span(t)], f"s2{t}")
        total = psb[t, span(t), :]
        for k in range(1, npr):
            total = total + psbr[t, k, span(t), :]
        psc[t, span(t), :] = total

    def sum_drain(t):
        gone(psa.at[t, pl.ds(1, ndp - 1), span(t)], f"s1{t}")
        gone(psbr.at[t, others, span(t)], f"s2{t}")

    def spread(t, at, fn, slot):
        for j in range(tiles):
            v = fn(psc[t, at * part_rows + j : at * part_rows + j + 1, :])
            wb[pl.ds(8 * slot, 8), j * 128 : (j + 1) * 128] = jnp.broadcast_to(v, (8, 128))

    def next_weight(v):
        return 1.0 / (crops * v)

    tokens_start(0)
    ps1[...] = jnp.zeros_like(ps1)
    colb[...] = jnp.zeros_like(colb)
    for load in loads[2:]:
        load.wait()
    tokens_forward(0)
    ptr[...] = protos[...].astype(F32).T.astype(BF16)
    tokens_wait(0)
    head(0)
    raw_send(0)
    raw_finish(0)
    ag_first(0)
    tokens_start(1)
    ag_second(0)
    tokens_forward(1)
    ag_third(0)
    teacher_scores(c)
    ag_wait(0)
    teacher_scores(1 - c)
    tokens_wait(1)
    head(1)
    raw_send(1)
    first_scales()
    row_pass(False)
    put_rows(0, 0)
    sum_send(0)
    sum_middle(0)
    raw_finish(1)
    ag_first(1)
    sum_finish(0)
    spread(0, 0, next_weight, 0)
    row_pass(True)
    put_rows(1, 0)
    sum_send(1)
    ag_second(1)
    sum_middle(1)
    ag_third(1)
    rows8[...] = jnp.zeros_like(rows8)
    student_scores(c)
    ag_wait(1)
    student_scores(1 - c)
    put_rows(2, 1)
    sum_finish(1)
    spread(1, 0, next_weight, 0)
    row_pass(True)
    put_rows(2, 0)
    sum_send(2)
    sum_middle(2)
    sum_finish(2)
    spread(2, 0, lambda v: 1.0 / v, 0)
    spread(2, 1, lambda v: jnp.log(v) * LOG2E, 1)

    gp_out[...] = jnp.zeros_like(gp_out)
    losst[...] = jnp.zeros_like(losst)
    share = 1.0 / (crops * STUDENT_TEMP)

    def group_grads(zz, cc):
        lane0 = pl.multiple_of((zz * 2 + cc) * group, group)
        u = units[1, zz, cc].reshape(group, cols)

        def step(b):
            base = pl.multiple_of(b * pb, pb)
            r = pl.ds(base, pb)
            lossa = jnp.zeros((8, 128), F32)
            for j in range(gtiles):
                lanes = pl.ds(pl.multiple_of(lane0 + j * 128, 128), 128)
                inv, norm = wb[0:8, lanes], wb[8:16, lanes]
                for a in range(0, pb, 16):
                    outs = []
                    for h in (0, 8):
                        rr = pl.ds(base + a + h, 8)
                        tgt = ex[rr, lanes] * colb[rr, :] * inv
                        rel = lg2[rr, lanes] - norm
                        lossa = lossa - tgt * rel
                        outs.append((jnp.exp2(rel) - tgt) * share)
                    gt[pl.ds(base + a, 16), j * 128 : (j + 1) * 128] = jnp.concatenate(outs, axis=0).astype(BF16)
            losst[...] += lossa
            gp_out[r, :] += jnp.dot(gt[r, :], u, preferred_element_type=F32)

        loop(0, nb, step, unroll=nb)
        ugt[...] = jnp.dot(ptr[...], gt[...], preferred_element_type=F32)
        return ugt[...].T.reshape(2, group // 2, cols)

    planes = sorted(range(1, nz), key=lambda k: -min(k, nz - k)) + [0]
    for n, k in enumerate(planes):
        zz = ring(z + k, nz)
        sibs[n] = group_grads(zz, 1 - c)
        started(sibs.at[n], sibr.at[n], "g0", sib, me, n)
        mine = group_grads(zz, c)
        arrived(sibr.at[n], "g0", n)
        part[k] = mine + sibr[n]
        if k:
            for h in range(2):
                started(part.at[k, h, :, lo], zrecv.at[h, k - 1], "gz", zz * 2 + c, me, h)

        def send(m, k=k):
            to = ring(me + m, npr)
            if k:
                started(part.at[k, :, hrows(to), hi], precv.at[m, k - 1], "gp", dp, to)
            else:
                started(part.at[k, :, hrows(to), hi], ohr.at[m], "go", dp, to)

        loop(1, npr, send)

    for h in range(2):
        arrived(zrecv.at[h], "gz", h)
        total = part[0, h, :, lo]
        for k in range(nz - 1):
            total = total + zrecv[h, k]
        a2[h] = total

        def send(k, h=h):
            to = ring(me + k, npr)
            started(a2.at[h, hrows(to)], a2r.at[k, h], "ga", dp, to)

        loop(1, npr, send)
        if h == 0:
            arrived(precv.at[others], "gp")
            total = part[pl.ds(1, nz - 1), :, hrows(me), hi]
            for k in range(1, npr):
                total = total + precv[k]
            b2[...] = total
            for k in range(1, nz):
                started(b2.at[k - 1], b2r.at[k - 1], "gb", ring(z + k, nz) * 2 + c, me)

    losst[...] = losst[...] * (LN2 / crops)
    loop(1, npr, lambda k: started(losst, lossr.at[k], "l1", dp, ring(me + k, npr)))

    arrived(ohr.at[others], "go")
    grad_hi = part[0, :, hrows(me), hi]
    for k in range(1, npr):
        grad_hi = grad_hi + ohr[k]
    arrived(b2r, "gb")
    for k in range(nz - 1):
        grad_hi = grad_hi + b2r[k]
    arrived(a2r.at[others], "ga")
    grad_lo = a2[:, hrows(me), :]
    for k in range(1, npr):
        grad_lo = grad_lo + a2r[k]

    unit_grad = jnp.concatenate([grad_lo.reshape(rb, half), grad_hi.reshape(rb, half)], axis=1)
    own = own_float[...]
    along = jnp.sum(own * unit_grad, axis=1, keepdims=True)
    rg[rows(me), :] = ((unit_grad - own * along) * own_scale[...]).astype(BF16)
    loop(1, npr, lambda k: started(rg.at[rows(me)], rg.at[rows(me)], "r1", dp, ring(me + k, npr)))

    arrived(lossr.at[others], "l1")
    total = losst[...]
    for k in range(1, npr):
        total = total + lossr[k]
    lossd[...] = total
    loop(1, ndp, lambda k: started(lossd, lossdr.at[k], "l2", ring(dp + k, ndp), me))
    pre_s[...] = gelu_slope(pre_s[...])

    arrived(rg.at[pl.ds(0, (npr - 1) * rb)], "r1")
    raw_grad = rg[...]
    pre_grad = (nt_dot(raw_grad, w2s[...]) * pre_s[...]).astype(BF16)
    whole = gw.shape[0]
    parts = 2
    share_rows, piece = whole // (2 * parts), whole // (ndp * parts)

    def half_of(n, cc):
        return pl.ds(pl.multiple_of((2 * n + cc) * share_rows, 8), share_rows)

    def piece_of(n, zz):
        return pl.ds(pl.multiple_of((2 * n + c) * share_rows + zz * piece, 8), piece)

    wchunk = min(width, 256)
    sent = 0
    for i in range(width // wchunk + 1):
        if i < width // wchunk:
            sl = slice(i * wchunk, (i + 1) * wchunk)
            gw[sl, :] = tn_dot(tok[1, :, sl], pre_grad)
            done = (i + 1) * wchunk
        else:
            w2g = tn_dot(hid_s[...], raw_grad)
            gw[pl.ds(width, hb), :] = w2g[:, :hb]
            gw[pl.ds(width + hb, hb), :] = w2g[:, hb:]
            done = whole
        while sent < parts and done >= 2 * (sent + 1) * share_rows:
            started(gw.at[half_of(sent, 1 - c)], gwr.at[sent], "w0", sib, me, sent)
            sent += 1

    zpeers = pl.ds(1, nz - 1)
    for n in range(parts):
        arrived(gwr.at[n], "w0", n)
        gw[half_of(n, c), :] += gwr[n]
        for k in range(1, nz):
            zz = ring(z + k, nz)
            started(gw.at[piece_of(n, zz)], gwz.at[n, k], "w1", zz * 2 + c, me, n)
    for n in range(parts):
        total = gw[piece_of(n, z), :]
        arrived(gwz.at[n, zpeers], "w1", n)
        for k in range(1, nz):
            total = total + gwz[n, k]
        fw[piece_of(n, z), :] = total
        for k in range(1, nz):
            started(fw.at[piece_of(n, z)], fw.at[piece_of(n, z)], "w2", ring(z + k, nz) * 2 + c, me, n)
    for n in range(parts):
        arrived(gwz.at[n, zpeers], "w2", n)
        started(fw.at[half_of(n, c)], fw.at[half_of(n, c)], "w3", sib, me)

    arrived(lossdr.at[pl.ds(1, ndp - 1)], "l2")
    loss = lossd[...]
    for k in range(1, ndp):
        loss = loss + lossdr[k]
    loss_out[...] = jnp.sum(jnp.sum(loss, axis=0, keepdims=True), axis=1, keepdims=True)

    for v in (0, 1):
        tokens_drain(v)
        raw_drain(v)
        ag_drain(v)
    for t in range(3):
        sum_drain(t)
    gone(sibs, "g0")
    gone(zrecv, "gz")
    gone(ohr.at[others], "go")
    gone(precv.at[others], "gp")
    gone(a2r.at[others], "ga")
    gone(b2r, "gb")
    gone(lossr.at[others], "l1")
    gone(lossdr.at[pl.ds(1, ndp - 1)], "l2")
    gone(rg.at[pl.ds(0, (npr - 1) * rb)], "r1")
    gone(gwr, "w0")
    gone(gwz.at[:, zpeers], "w1")
    gone(gwz.at[:, zpeers], "w2")

    arrived(gwr, "w3")
    gw1_out[...] = fw[:width, :]
    gw2_out[:, :hb] = fw[width : width + hb, :]
    gw2_out[:, hb:] = fw[width + hb :, :]
    gone(gwr, "w3")


def step(dims, s_in, t_in, w1s, w2s, w1t, w2t, protos):
    nz, nx, ny = dims["nz"], dims["nx"], dims["ny"]
    ndp, npr = 2 * nz, nx * ny
    rb, width = s_in.shape
    hb, cols = w2s.shape
    kp = protos.shape[0]
    group = rb * npr
    crops = group * ndp
    half = cols // 2
    dims = dict(dims, rb=rb, q=group // 128)

    plan, n_send, n_recv = {}, 0, 0
    phases = [(f"{name}{v}", n) for v in (0, 1) for name, n in dict(
        tx=nx, ty=ny, fa=1, fb=1, rr=1, a1=1, b1=1, b2=nx, a2=nz, d1=nz, sa=1, sb=1, sd=1).items()]
    phases += [(f"{name}{t}", 1) for t in range(3) for name in ("s1", "s2")]
    phases += [("g0", nz), ("gz", 2), ("w0", 2), ("w1", 2), ("w2", 2)]
    phases += [(n, 1) for n in ("gp", "go", "ga", "gb", "l1", "l2", "r1", "w3")]
    for name, n in phases:
        plan[name] = (n_send, n_recv)
        n_send, n_recv = n_send + 1, n_recv + n
    part_rows = max(8, crops // 128)

    wrows = width + 2 * hb
    V = pltpu.VMEM
    scratch = [
        V((width, hb), BF16),
        V((hb, cols), BF16),
        V((width, hb), BF16),
        V((hb, cols), BF16),
        V((kp, cols), BF16),
        V((2, group, width), BF16),
        V((group, hb), F32),
        V((group, hb), BF16),
        V((2, group, cols), F32),
        V((2, npr, rb, cols), F32),
        V((2, nz, 2, 2, group // 2, cols), BF16),
        V((rb, cols), F32),
        V((rb, 1), F32),
        V((kp, crops), F32),
        V((kp, crops), F32),
        V((kp, 128), F32),
        V((16, crops), F32),
        V((8, crops), F32),
        V((3, 2 * part_rows, 128), F32),
        V((3, ndp, 2 * part_rows, 128), F32),
        V((3, 2 * part_rows, 128), F32),
        V((3, npr, 2 * part_rows, 128), F32),
        V((3, 2 * part_rows, 128), F32),
        V((kp, group), BF16),
        V((cols, kp), BF16),
        V((cols, group), F32),
        V((nz, 2, group // 2, cols), F32),
        V((nz, 2, group // 2, cols), F32),
        V((nz, 2, group // 2, cols), F32),
        V((2, nz - 1, group // 2, half), F32),
        V((npr, nz - 1, 2, rb // 2, half), F32),
        V((npr, 2, rb // 2, half), F32),
        V((2, group // 2, half), F32),
        V((npr, 2, rb // 2, half), F32),
        V((nz - 1, 2, rb // 2, half), F32),
        V((nz - 1, 2, rb // 2, half), F32),
        V((8, 128), F32),
        V((npr, 8, 128), F32),
        V((8, 128), F32),
        V((ndp, 8, 128), F32),
        V((group, cols), BF16),
        V((wrows, hb), F32),
        V((2, wrows // 4, hb), F32),
        V((2, nz, wrows // (2 * ndp), hb), F32),
        V((wrows, hb), F32),
        pltpu.SemaphoreType.DMA((n_send,)),
        pltpu.SemaphoreType.DMA((n_recv,)),
        pltpu.SemaphoreType.DMA((7,)),
    ]
    vmem = pl.BlockSpec(memory_space=pltpu.VMEM)
    gp, gw1, gw2, loss = pl.pallas_call(
        functools.partial(kernel, dims, plan),
        out_shape=(
            pltpu.VMEM((kp, cols), F32),
            pltpu.VMEM((width, hb), F32),
            pltpu.VMEM((hb, cols), F32),
            jax.ShapeDtypeStruct((1, 1), F32),
        ),
        in_specs=[pl.BlockSpec(memory_space=pl.ANY)] * 7,
        out_specs=(vmem,) * 4,
        scratch_shapes=scratch,
        compiler_params=pltpu.CompilerParams(
            collective_id=0, has_side_effects=True, vmem_limit_bytes=61 * 1024 * 1024
        ),
        cost_estimate=pl.CostEstimate(
            flops=8 * kp * crops * cols, bytes_accessed=4 * kp * cols * 4, transcendentals=2 * kp * crops
        ),
    )(s_in, t_in, w1s, w2s, w1t, w2t, protos)
    return gp, gw1, gw2, loss[0, 0]


def solution(mesh):
    ndp, npr = mesh.shape["dp"], mesh.shape["proto"]
    side = math.isqrt(npr)
    dims = dict(nz=ndp // 2, nx=side, ny=npr // side)
    both = P(("dp", "proto"), None)
    return jax.shard_map(
        functools.partial(step, dims),
        mesh=mesh,
        in_specs=(both, both, P(None, "proto"), P("proto", None), P(None, "proto"), P("proto", None), both),
        out_specs=(both, P(None, "proto"), P("proto", None), P()),
        check_vma=False,
    )
```

```python
import functools
import math

import jax
import jax.numpy as jnp
from jax import lax
from jax.experimental import pallas as pl
from jax.experimental.pallas import tpu as pltpu
from jax.sharding import PartitionSpec as P

MESH = pl.DeviceIdType.MESH
TEACHER_TEMP = 0.07
STUDENT_TEMP = 0.1
LOG2E = 1.4426950408889634
LN2 = 0.6931471805599453
F32 = jnp.float32
BF16 = jnp.bfloat16


def normal_cdf(x):
    return 0.5 * (1.0 + lax.erf(x * (1.0 / math.sqrt(2.0))))


def gelu(x):
    return x * normal_cdf(x)


def gelu_slope(x):
    return normal_cdf(x) + x * (jnp.exp(-0.5 * x * x) * (1.0 / math.sqrt(2.0 * math.pi)))


def nt_dot(a, b):
    return lax.dot_general(a, b, (((1,), (1,)), ((), ())), preferred_element_type=F32)


def tn_dot(a, b):
    return lax.dot_general(a, b, (((0,), (0,)), ((), ())), preferred_element_type=F32)


def unit_scale(raw):
    return lax.rsqrt(jnp.sum(raw * raw, axis=1, keepdims=True) + 1e-06)


def kernel(dims, plan, s_in, t_in, w1s_in, w2s_in, w1t_in, w2t_in, protos_in, gp_out, gw1_out, gw2_out, loss_out, *scratch):
    nz, nx, ny, rb, q = dims["nz"], dims["nx"], dims["ny"], dims["rb"], dims["q"]
    ndp, npr = 2 * nz, nx * ny
    width, hb, cols, kp = w1s_in.shape[0], w1s_in.shape[1], w2s_in.shape[1], protos_in.shape[0]
    group = rb * npr
    crops = group * ndp
    total_protos = kp * ndp * npr
    tiles = crops // 128
    part_rows = max(8, tiles)
    half = cols // 2
    hr = rb // 2
    (w1s, w2s, w1g, w2g, protos, tok, pre_s, hid_s, rawp, rawr, units, own_float, own_scale, ex, lg2, colb, wb, rows8,
     ps1, psa, psb, psbr, psc, gt, ptr, ugt, sibs, sibr, part, zrecv, precv, ohr, a2, a2r, b2, b2r, losst, lossr, lossd,
     lossdr, rg, gw, gwr, gwz, fw, ssem, rsem, lsem) = scratch

    dp, me = lax.axis_index("dp"), lax.axis_index("proto")
    z, c = dp // 2, dp % 2
    x, y = me // ny, me % ny

    def started(src, dst, name, to_dp, to_proto, nth=0, send_as=None):
        s, r = plan[send_as or name][0], plan[name][1]
        pltpu.make_async_remote_copy(
            src_ref=src, dst_ref=dst, send_sem=ssem.at[s], recv_sem=rsem.at[r + nth],
            device_id=(to_dp, to_proto), device_id_type=MESH,
        ).start()

    def arrived(dst, name, nth=0):
        pltpu.make_async_copy(dst, dst, rsem.at[plan[name][1] + nth]).wait()

    def gone(src, name):
        pltpu.make_async_copy(src, src, ssem.at[plan[name][0]]).wait()

    def loop(lo, hi, fn, unroll=1):
        def step(k, carry):
            fn(k)
            return carry

        lax.fori_loop(lo, hi, step, 0, unroll=unroll)

    def proto_of(xx, yy):
        return lax.rem(xx + nx, nx) * ny + lax.rem(yy + ny, ny)

    def rows(p):
        return pl.ds(pl.multiple_of(p * rb, rb), rb)

    def hrows(p):
        return pl.ds(pl.multiple_of(p * hr, hr), hr)

    def ring(value, n):
        return lax.rem(value + n, n)

    left, right = pl.ds(0, width // 2), pl.ds(width // 2, width // 2)
    lo, hi = pl.ds(0, half), pl.ds(half, half)
    sib = dp + 1 - 2 * c

    ny2 = ny // 2

    def w1_slot(s):
        return w1g.at[:, pl.ds(pl.multiple_of(s * hb, hb), hb)]

    def w2_slot(s):
        return w2g.at[pl.ds(pl.multiple_of(s * hb, hb), hb)]

    loads = [
        pltpu.make_async_copy(src, dst, lsem.at[n])
        for n, (src, dst) in enumerate(
            [(t_in, tok.at[0, rows(c * nx + x)]), (s_in, tok.at[1, rows(me)]), (w1t_in, w1_slot(lax.rem(y, ny2))),
             (w2t_in, w2_slot(lax.rem(y, ny2))), (protos_in, protos), (w1s_in, w1s), (w2s_in, w2s)]
        )
    ]
    for n, load in enumerate(loads):
        if n not in (2, 3):
            load.start()

    @pl.when(y // ny2 == c)
    def _():
        loads[2].start()
        loads[3].start()

    barrier = pltpu.get_barrier_semaphore()

    def greet_proto(k):
        pl.semaphore_signal(barrier, inc=1, device_id=(dp, ring(me + k, npr)), device_id_type=MESH)

    def greet_dp(k):
        pl.semaphore_signal(barrier, inc=1, device_id=(ring(dp + k, ndp), me), device_id_type=MESH)

    loop(1, npr, greet_proto)
    loop(1, ndp, greet_dp)
    loads[0].wait()
    loads[1].wait()
    pl.semaphore_wait(barrier, npr - 1 + ndp - 1)

    def front_start():
        mine = tok.at[0, rows(c * nx + x)]
        for k in range(1, nx):
            started(mine, mine, "tx0", dp, proto_of(x + k, y), k)
        started(mine, mine, "ts0", sib, me)

        @pl.when(y // ny2 == c)
        def _():
            s = lax.rem(y, ny2)
            loads[2].wait()
            for k in range(1, ny):
                started(w1_slot(s), w1_slot(s), "v1", dp, proto_of(x, y + k), s, f"v1s{k}")
            loads[3].wait()
            for k in range(1, ny):
                started(w2_slot(s), w2_slot(s), "v2", dp, proto_of(x, y + k), s, f"v2s{k}")

    def front_forward():
        for k in range(1, nx):
            block = tok.at[0, rows(c * nx + lax.rem(x - k + nx, nx))]
            arrived(block, "tx0", k)
            started(block, block, "ts0", sib, me)

    def front_wait():
        arrived(tok.at[0, pl.ds(pl.multiple_of((1 - c) * (nx * rb), nx * rb), nx * rb)], "ts0")
        for s in range(ny2):

            @pl.when(c * ny2 + s != y)
            def _(s=s):
                arrived(w1_slot(s), "v1", s)
                arrived(w2_slot(s), "v2", s)

    def front_drain():
        gone(tok.at[0, pl.ds(0, (nx - 1) * rb)], "tx0")
        gone(tok.at[0, pl.ds(0, nx * rb)], "ts0")

        @pl.when(y // ny2 == c)
        def _():
            for k in range(1, ny):
                gone(w1_slot(0), f"v1s{k}")
                gone(w2_slot(0), f"v2s{k}")

    def front_head():
        r = pl.ds(0, 2 * nx * rb)
        pre = jnp.dot(tok[0, r, :], w1g[...], preferred_element_type=F32)
        rawp[0, r, :] = jnp.dot(gelu(pre).astype(BF16), w2g[...], preferred_element_type=F32)

    def front_raw_send():
        for kc in range(2):
            for kx in range(nx):
                if kc or kx:
                    cc, xx = c + kc - 2 * c * kc, lax.rem(x + kx, nx)
                    started(rawp.at[0, rows(cc * nx + xx)], rawr.at[0, kc * nx + kx], "rr0", 2 * z + cc, proto_of(xx, y))

    def front_raw_finish():
        arrived(rawr.at[0, pl.ds(1, 2 * nx - 1)], "rr0")
        raw = rawp[0, rows(c * nx + x), :]
        for k in range(1, 2 * nx):
            raw = raw + rawr[0, k]
        put_unit(0, raw)

    def front_raw_drain():
        gone(rawr.at[0, pl.ds(1, 2 * nx - 1)], "rr0")

    def put_unit(v, raw):
        scale = unit_scale(raw)
        unit_float = raw * scale
        if v == 1:
            own_float[...] = unit_float
            own_scale[...] = scale
        units[v, z, c, :, hrows(me), :] = unit_float.astype(BF16).reshape(2, hr, cols)

    def tokens_start_x(v):
        mine = tok.at[v, rows(me)]
        for k in range(1, nx):
            started(mine, mine, f"tx{v}", dp, proto_of(x + k, y), k)

    def tokens_start_y(v):
        mine = tok.at[v, rows(me)]
        for k in range(1, ny):
            started(mine, mine, f"ty{v}", dp, proto_of(x, y + k), k)

    def tokens_forward_y(v):
        for k in range(1, nx):
            block = rows(proto_of(x - k, y))
            arrived(tok.at[v, block], f"tx{v}", k)
            ref = tok.at[v, block, left]
            for m in range(1, ny):
                started(ref, ref, f"fa{v}", dp, proto_of(x, y + m))

    def tokens_forward_x(v):
        for k in range(1, ny):
            block = rows(proto_of(x, y - k))
            arrived(tok.at[v, block], f"ty{v}", k)
            ref = tok.at[v, block, right]
            for m in range(1, nx):
                started(ref, ref, f"fb{v}", dp, proto_of(x + m, y))

    diagonal = pl.ds(0, (nx - 1) * (ny - 1) * rb)

    def tokens_wait(v):
        arrived(tok.at[v, diagonal, left], f"fa{v}")
        arrived(tok.at[v, diagonal, right], f"fb{v}")

    def tokens_drain(v):
        gone(tok.at[v, pl.ds(0, (nx - 1) * rb)], f"tx{v}")
        gone(tok.at[v, pl.ds(0, (ny - 1) * rb)], f"ty{v}")
        gone(tok.at[v, diagonal, left], f"fa{v}")
        gone(tok.at[v, diagonal, right], f"fb{v}")

    def head(v):
        step = min(group, 256)

        def chunk(i):
            r = pl.ds(pl.multiple_of(i * step, step), step)
            pre = jnp.dot(tok[v, r, :], w1s[...], preferred_element_type=F32)
            hidden = gelu(pre).astype(BF16)
            pre_s[r, :] = pre
            hid_s[r, :] = hidden
            rawp[v, r, :] = jnp.dot(hidden, w2s[...], preferred_element_type=F32)

        loop(0, group // step, chunk, unroll=group // step)

    def raw_send(v):
        def send(k):
            to = ring(me + k, npr)
            started(rawp.at[v, rows(to)], rawr.at[v, k], f"rr{v}", dp, to)

        loop(1, npr, send)

    others = pl.ds(1, npr - 1)

    def raw_finish(v):
        arrived(rawr.at[v, others], f"rr{v}")
        raw = rawp[v, rows(me), :]
        for k in range(1, npr):
            raw = raw + rawr[v, k]
        put_unit(v, raw)

    def raw_drain(v):
        gone(rawr.at[v, others], f"rr{v}")

    def band(xx):
        return pl.ds(pl.multiple_of(ring(xx, nx) * (ny * hr), ny * hr), ny * hr)

    def ag_first(v):
        mine = units.at[v, z, c, 1, hrows(me)]
        for k in range(1, nz):
            started(mine.at[:, hi], mine.at[:, hi], f"b1{v}", ring(z + k, nz) * 2 + c, me)
        loop(1, npr, lambda k: started(mine.at[:, lo], mine.at[:, lo], f"a1{v}", dp, ring(me + k, npr)))
        direct = units.at[v, z, c, 0, hrows(me)]
        for kz in list(range(1, nz)) + [0]:

            def send(k, kz=kz):
                started(direct, direct, f"d1{v}", ring(z + kz, nz) * 2 + c, ring(me + k, npr), kz)

            loop(0 if kz else 1, npr, send)

    def ag_second(v):
        arrived(units.at[v, pl.ds(0, nz - 1), c, 1, hrows(me), hi], f"b1{v}")
        col = units.at[v, :, c, 1, hrows(me), hi]
        for kx in range(nx):
            for ky in range(ny):
                if kx or ky:
                    started(col, col, f"b2{v}", dp, proto_of(x + kx, y + ky), kx)
        arrived(units.at[v, z, c, 1, pl.ds(0, (npr - 1) * hr), lo], f"a1{v}")
        plane = units.at[v, z, c, 1, :, lo]
        for k in range(1, nz):
            started(plane, plane, f"a2{v}", ring(z + k, nz) * 2 + c, me, k)
        started(plane, plane, f"sa{v}", sib, me)

    def ag_third(v):
        for k in range(nz):
            plane = units.at[v, ring(z - k, nz), c, 0]
            if k:
                arrived(plane, f"d1{v}", k)
            else:
                arrived(units.at[v, z, c, 0, pl.ds(0, (npr - 1) * hr)], f"d1{v}", k)
            started(plane, plane, f"sd{v}", sib, me)
        for k in range(1, nz):
            plane = units.at[v, ring(z - k, nz), c, 1, :, lo]
            arrived(plane, f"a2{v}", k)
            started(plane, plane, f"sa{v}", sib, me)
        for k in range(nx):
            piece = units.at[v, :, c, 1, band(x - k), hi]
            if k:
                arrived(piece, f"b2{v}", k)
            else:
                arrived(units.at[v, :, c, 1, pl.ds(0, (ny - 1) * hr), hi], f"b2{v}", k)
            started(piece, piece, f"sb{v}", sib, me)

    def ag_wait(v):
        arrived(units.at[v, :, 1 - c, 0], f"sd{v}")
        arrived(units.at[v, :, 1 - c, 1, :, lo], f"sa{v}")
        arrived(units.at[v, :, 1 - c, 1, :, hi], f"sb{v}")

    def ag_drain(v):
        gone(protos.at[pl.ds(0, (nz * npr - 1) * hr)], f"d1{v}")
        gone(units.at[v, :, c, 0], f"sd{v}")
        gone(units.at[v, z, c, 1, pl.ds(0, (npr - 1) * hr), lo], f"a1{v}")
        gone(units.at[v, pl.ds(0, nz - 1), c, 1, hrows(me), hi], f"b1{v}")
        gone(units.at[v, :, c, 1, pl.ds(0, (npr - 1) * hr), hi], f"b2{v}")
        gone(units.at[v, pl.ds(0, nz - 1), c, 1, :, lo], f"a2{v}")
        gone(units.at[v, :, c, 1, :, lo], f"sa{v}")
        gone(units.at[v, :, c, 1, :, hi], f"sb{v}")

    def slow_first(v):
        mine = units.at[v, z, c, :, hrows(me)]
        for k in range(1, nz):
            started(mine.at[:, :, hi], mine.at[:, :, hi], f"b1{v}", ring(z + k, nz) * 2 + c, me)
        loop(1, npr, lambda k: started(mine.at[:, :, lo], mine.at[:, :, lo], f"a1{v}", dp, ring(me + k, npr)))

    def slow_second_z(v):
        arrived(units.at[v, z, c, :, pl.ds(0, (npr - 1) * hr), lo], f"a1{v}")
        plane = units.at[v, z, c, :, :, lo]
        for k in range(1, nz):
            started(plane, plane, f"a2{v}", ring(z + k, nz) * 2 + c, me, k)
        started(plane, plane, f"sa{v}", sib, me)

    def slow_second_proto(v):
        arrived(units.at[v, pl.ds(0, nz - 1), c, :, hrows(me), hi], f"b1{v}")
        col = units.at[v, :, c, :, hrows(me), hi]
        for kx in range(nx):
            for ky in range(ny):
                if kx or ky:
                    started(col, col, f"b2{v}", dp, proto_of(x + kx, y + ky), kx)

    def slow_third(v):
        for k in range(1, nz):
            plane = units.at[v, ring(z - k, nz), c, :, :, lo]
            arrived(plane, f"a2{v}", k)
            started(plane, plane, f"sa{v}", sib, me)
        for k in range(nx):
            piece = units.at[v, :, c, :, band(x - k), hi]
            if k:
                arrived(piece, f"b2{v}", k)
            else:
                arrived(units.at[v, :, c, :, pl.ds(0, (ny - 1) * hr), hi], f"b2{v}", k)
            started(piece, piece, f"sb{v}", sib, me)

    def slow_wait(v):
        arrived(units.at[v, :, 1 - c, :, :, lo], f"sa{v}")
        arrived(units.at[v, :, 1 - c, :, :, hi], f"sb{v}")

    def slow_drain(v):
        gone(units.at[v, z, c, :, pl.ds(0, (npr - 1) * hr), lo], f"a1{v}")
        gone(units.at[v, pl.ds(0, nz - 1), c, :, hrows(me), hi], f"b1{v}")
        gone(units.at[v, :, c, :, pl.ds(0, (npr - 1) * hr), hi], f"b2{v}")
        gone(units.at[v, pl.ds(0, nz - 1), c, :, :, lo], f"a2{v}")
        gone(units.at[v, :, c, :, :, lo], f"sa{v}")
        gone(units.at[v, :, c, :, :, hi], f"sb{v}")

    pb = min(kp, 256)
    nb = kp // pb
    gtiles = group // 128

    def teacher_scores(cc):
        def step(i):
            zz, b = i // nb, i % nb
            r = pl.ds(pl.multiple_of(b * pb, pb), pb)
            s = nt_dot(protos[r, :], units[0, zz, cc].reshape(group, cols))
            e = jnp.exp2(s * (LOG2E / TEACHER_TEMP))
            ex[r, pl.ds(pl.multiple_of((2 * zz + cc) * group, group), group)] = e
            acc = e[:, :128]
            for j in range(1, gtiles):
                acc = acc + e[:, j * 128 : (j + 1) * 128]
            colb[r, :] += acc

        loop(0, nz * nb, step, unroll=2 * nb)

    def first_scales():
        def scale(i):
            r = pl.ds(pl.multiple_of(i * 64, 64), 64)
            total = jnp.sum(colb[r, :], axis=1, keepdims=True)
            colb[r, :] = jnp.broadcast_to(1.0 / (total_protos * total), (64, 128))

        loop(0, kp // 64, scale, unroll=2)

    def student_scores(cc):
        def step(i):
            zz, b = i // nb, i % nb
            r = pl.ds(pl.multiple_of(b * pb, pb), pb)
            lanes = pl.ds(pl.multiple_of((2 * zz + cc) * group, group), group)
            s = nt_dot(protos[r, :], units[1, zz, cc].reshape(group, cols)) * (LOG2E / STUDENT_TEMP)
            lg2[r, lanes] = s
            rows8[:, lanes] += jnp.sum(jnp.exp2(s).reshape(pb // 8, 8, group), axis=0)

        loop(0, nz * nb, step, unroll=2 * nb)

    def row_pass(fresh):
        rows8[...] = jnp.zeros_like(rows8)

        def step(i):
            base = pl.multiple_of(i * 64, 64)
            if fresh:
                accs = [None] * 8
                for j in range(tiles):
                    lanes = slice(j * 128, (j + 1) * 128)
                    w = wb[0:8, lanes]
                    for a in range(8):
                        term = ex[pl.ds(base + 8 * a, 8), lanes] * w
                        accs[a] = term if accs[a] is None else accs[a] + term
                scales = []
                for a in range(8):
                    total = jnp.sum(accs[a], axis=1, keepdims=True)
                    scale = jnp.broadcast_to(1.0 / (total_protos * total), (8, 128))
                    colb[pl.ds(base + 8 * a, 8), :] = scale
                    scales.append(scale)
            else:
                scales = [colb[pl.ds(base + 8 * a, 8), :] for a in range(8)]
            for j in range(tiles):
                lanes = slice(j * 128, (j + 1) * 128)
                terms = [ex[pl.ds(base + 8 * a, 8), lanes] * scales[a] for a in range(8)]
                while len(terms) > 1:
                    terms = [terms[n] + terms[n + 1] for n in range(0, len(terms), 2)]
                rows8[:, lanes] += terms[0]

        loop(0, kp // 64, step, unroll=2)

    def put_rows(t, at):
        for j in range(tiles):
            ps1[t, at * part_rows + j : at * part_rows + j + 1, :] = jnp.sum(
                rows8[:, j * 128 : (j + 1) * 128], axis=0, keepdims=True
            )

    def span(t):
        return pl.ds(0, part_rows * (2 if t == 2 else 1))

    def sum_send(t):
        for k in range(1, ndp):
            started(ps1.at[t, span(t)], psa.at[t, k, span(t)], f"s1{t}", ring(dp + k, ndp), me)

    def sum_middle(t):
        arrived(psa.at[t, pl.ds(1, ndp - 1), span(t)], f"s1{t}")
        total = ps1[t, span(t), :]
        for k in range(1, ndp):
            total = total + psa[t, k, span(t), :]
        psb[t, span(t), :] = total
        for k in range(1, npr):
            started(psb.at[t, span(t)], psbr.at[t, k, span(t)], f"s2{t}", dp, ring(me + k, npr))

    def sum_finish(t):
        arrived(psbr.at[t, others, span(t)], f"s2{t}")
        total = psb[t, span(t), :]
        for k in range(1, npr):
            total = total + psbr[t, k, span(t), :]
        psc[t, span(t), :] = total

    def sum_drain(t):
        gone(psa.at[t, pl.ds(1, ndp - 1), span(t)], f"s1{t}")
        gone(psbr.at[t, others, span(t)], f"s2{t}")

    def spread(t, at, fn, slot):
        for j in range(tiles):
            v = fn(psc[t, at * part_rows + j : at * part_rows + j + 1, :])
            wb[pl.ds(8 * slot, 8), j * 128 : (j + 1) * 128] = jnp.broadcast_to(v, (8, 128))

    def next_weight(v):
        return 1.0 / (crops * v)

    front_start()
    tokens_start_x(1)
    tokens_start_y(1)
    ps1[...] = jnp.zeros_like(ps1)
    colb[...] = jnp.zeros_like(colb)
    for load in loads[4:]:
        load.wait()
    front_forward()
    ptr[...] = protos[...].astype(F32).T.astype(BF16)
    front_wait()
    front_head()
    front_raw_send()
    tokens_forward_y(1)
    tokens_forward_x(1)
    front_raw_finish()
    ag_first(0)
    ag_second(0)
    tokens_wait(1)
    head(1)
    ag_third(0)
    raw_send(1)
    teacher_scores(c)
    ag_wait(0)
    teacher_scores(1 - c)
    first_scales()
    row_pass(False)
    put_rows(0, 0)
    sum_send(0)
    raw_finish(1)
    slow_first(1)
    sum_middle(0)
    slow_second_z(1)
    sum_finish(0)
    spread(0, 0, next_weight, 0)
    slow_second_proto(1)
    row_pass(True)
    put_rows(1, 0)
    sum_send(1)
    sum_middle(1)
    slow_third(1)
    rows8[...] = jnp.zeros_like(rows8)
    student_scores(c)
    slow_wait(1)
    student_scores(1 - c)
    put_rows(2, 1)
    sum_finish(1)
    spread(1, 0, next_weight, 0)
    row_pass(True)
    put_rows(2, 0)
    sum_send(2)
    sum_middle(2)
    sum_finish(2)
    spread(2, 0, lambda v: 1.0 / v, 0)
    spread(2, 1, lambda v: jnp.log(v) * LOG2E, 1)

    gp_out[...] = jnp.zeros_like(gp_out)
    losst[...] = jnp.zeros_like(losst)
    share = 1.0 / (crops * STUDENT_TEMP)

    def group_grads(zz, cc):
        lane0 = pl.multiple_of((zz * 2 + cc) * group, group)
        u = units[1, zz, cc].reshape(group, cols)

        def step(b):
            base = pl.multiple_of(b * pb, pb)
            r = pl.ds(base, pb)
            lossa = jnp.zeros((8, 128), F32)
            for j in range(gtiles):
                lanes = pl.ds(pl.multiple_of(lane0 + j * 128, 128), 128)
                inv, norm = wb[0:8, lanes], wb[8:16, lanes]
                for a in range(0, pb, 16):
                    outs = []
                    for h in (0, 8):
                        rr = pl.ds(base + a + h, 8)
                        tgt = ex[rr, lanes] * colb[rr, :] * inv
                        rel = lg2[rr, lanes] - norm
                        lossa = lossa - tgt * rel
                        outs.append((jnp.exp2(rel) - tgt) * share)
                    gt[pl.ds(base + a, 16), j * 128 : (j + 1) * 128] = jnp.concatenate(outs, axis=0).astype(BF16)
            losst[...] += lossa
            gp_out[r, :] += jnp.dot(gt[r, :], u, preferred_element_type=F32)

        loop(0, nb, step, unroll=nb)
        ugt[...] = jnp.dot(ptr[...], gt[...], preferred_element_type=F32)
        return ugt[...].T.reshape(2, group // 2, cols)

    planes = sorted(range(1, nz), key=lambda k: -min(k, nz - k)) + [0]
    for n, k in enumerate(planes):
        zz = ring(z + k, nz)
        sibs[n] = group_grads(zz, 1 - c)
        started(sibs.at[n], sibr.at[n], "g0", sib, me, n)
        mine = group_grads(zz, c)
        arrived(sibr.at[n], "g0", n)
        part[k] = mine + sibr[n]
        if k:
            for h in range(2):
                started(part.at[k, h, :, lo], zrecv.at[h, k - 1], "gz", zz * 2 + c, me, h)

        def send(m, k=k):
            to = ring(me + m, npr)
            if k:
                started(part.at[k, :, hrows(to), hi], precv.at[m, k - 1], "gp", dp, to)
            else:
                started(part.at[k, :, hrows(to), hi], ohr.at[m], "go", dp, to)

        loop(1, npr, send)

    for h in range(2):
        arrived(zrecv.at[h], "gz", h)
        total = part[0, h, :, lo]
        for k in range(nz - 1):
            total = total + zrecv[h, k]
        a2[h] = total

        def send(k, h=h):
            to = ring(me + k, npr)
            started(a2.at[h, hrows(to)], a2r.at[k, h], "ga", dp, to)

        loop(1, npr, send)
        if h == 0:
            arrived(precv.at[others], "gp")
            total = part[pl.ds(1, nz - 1), :, hrows(me), hi]
            for k in range(1, npr):
                total = total + precv[k]
            b2[...] = total
            for k in range(1, nz):
                started(b2.at[k - 1], b2r.at[k - 1], "gb", ring(z + k, nz) * 2 + c, me)

    losst[...] = losst[...] * (LN2 / crops)
    loop(1, npr, lambda k: started(losst, lossr.at[k], "l1", dp, ring(me + k, npr)))

    arrived(ohr.at[others], "go")
    grad_hi = part[0, :, hrows(me), hi]
    for k in range(1, npr):
        grad_hi = grad_hi + ohr[k]
    arrived(b2r, "gb")
    for k in range(nz - 1):
        grad_hi = grad_hi + b2r[k]
    arrived(a2r.at[others], "ga")
    grad_lo = a2[:, hrows(me), :]
    for k in range(1, npr):
        grad_lo = grad_lo + a2r[k]

    unit_grad = jnp.concatenate([grad_lo.reshape(rb, half), grad_hi.reshape(rb, half)], axis=1)
    own = own_float[...]
    along = jnp.sum(own * unit_grad, axis=1, keepdims=True)
    rg[rows(me), :] = ((unit_grad - own * along) * own_scale[...]).astype(BF16)
    loop(1, npr, lambda k: started(rg.at[rows(me)], rg.at[rows(me)], "r1", dp, ring(me + k, npr)))

    arrived(lossr.at[others], "l1")
    total = losst[...]
    for k in range(1, npr):
        total = total + lossr[k]
    lossd[...] = total
    loop(1, ndp, lambda k: started(lossd, lossdr.at[k], "l2", ring(dp + k, ndp), me))
    pre_s[...] = gelu_slope(pre_s[...])

    arrived(rg.at[pl.ds(0, (npr - 1) * rb)], "r1")
    raw_grad = rg[...]
    pre_grad = (nt_dot(raw_grad, w2s[...]) * pre_s[...]).astype(BF16)
    whole = gw.shape[0]
    parts = 2
    share_rows, piece = whole // (2 * parts), whole // (ndp * parts)

    def half_of(n, cc):
        return pl.ds(pl.multiple_of((2 * n + cc) * share_rows, 8), share_rows)

    def piece_of(n, zz):
        return pl.ds(pl.multiple_of((2 * n + c) * share_rows + zz * piece, 8), piece)

    wchunk = min(width, 256)
    sent = 0
    for i in range(width // wchunk + 1):
        if i < width // wchunk:
            sl = slice(i * wchunk, (i + 1) * wchunk)
            gw[sl, :] = tn_dot(tok[1, :, sl], pre_grad)
            done = (i + 1) * wchunk
        else:
            grad2 = tn_dot(hid_s[...], raw_grad)
            gw[pl.ds(width, hb), :] = grad2[:, :hb]
            gw[pl.ds(width + hb, hb), :] = grad2[:, hb:]
            done = whole
        while sent < parts and done >= 2 * (sent + 1) * share_rows:
            started(gw.at[half_of(sent, 1 - c)], gwr.at[sent], "w0", sib, me, sent)
            sent += 1

    zpeers = pl.ds(1, nz - 1)
    for n in range(parts):
        arrived(gwr.at[n], "w0", n)
        gw[half_of(n, c), :] += gwr[n]
        for k in range(1, nz):
            zz = ring(z + k, nz)
            started(gw.at[piece_of(n, zz)], gwz.at[n, k], "w1", zz * 2 + c, me, n)
    for n in range(parts):
        total = gw[piece_of(n, z), :]
        arrived(gwz.at[n, zpeers], "w1", n)
        for k in range(1, nz):
            total = total + gwz[n, k]
        fw[piece_of(n, z), :] = total
        for k in range(1, nz):
            started(fw.at[piece_of(n, z)], fw.at[piece_of(n, z)], "w2", ring(z + k, nz) * 2 + c, me, n)
    for n in range(parts):
        arrived(gwz.at[n, zpeers], "w2", n)
        started(fw.at[half_of(n, c)], fw.at[half_of(n, c)], "w3", sib, me)

    arrived(lossdr.at[pl.ds(1, ndp - 1)], "l2")
    loss = lossd[...]
    for k in range(1, ndp):
        loss = loss + lossdr[k]
    loss_out[...] = jnp.sum(jnp.sum(loss, axis=0, keepdims=True), axis=1, keepdims=True)

    front_drain()
    front_raw_drain()
    tokens_drain(1)
    raw_drain(1)
    ag_drain(0)
    slow_drain(1)
    for t in range(3):
        sum_drain(t)
    gone(sibs, "g0")
    gone(zrecv, "gz")
    gone(ohr.at[others], "go")
    gone(precv.at[others], "gp")
    gone(a2r.at[others], "ga")
    gone(b2r, "gb")
    gone(lossr.at[others], "l1")
    gone(lossdr.at[pl.ds(1, ndp - 1)], "l2")
    gone(rg.at[pl.ds(0, (npr - 1) * rb)], "r1")
    gone(gwr, "w0")
    gone(gwz.at[:, zpeers], "w1")
    gone(gwz.at[:, zpeers], "w2")

    arrived(gwr, "w3")
    gw1_out[...] = fw[:width, :]
    gw2_out[:, :hb] = fw[width : width + hb, :]
    gw2_out[:, hb:] = fw[width + hb :, :]
    gone(gwr, "w3")


def step(dims, s_in, t_in, w1s, w2s, w1t, w2t, protos):
    nz, nx, ny = dims["nz"], dims["nx"], dims["ny"]
    ndp, npr = 2 * nz, nx * ny
    rb, width = s_in.shape
    hb, cols = w2s.shape
    kp = protos.shape[0]
    group = rb * npr
    crops = group * ndp
    half = cols // 2
    dims = dict(dims, rb=rb, q=group // 128)

    plan, n_send, n_recv = {}, 0, 0
    phases = [(f"{name}{v}", n) for v in (0, 1) for name, n in dict(
        rr=1, a1=1, b1=1, b2=nx, a2=nz, d1=nz, sa=1, sb=1, sd=1).items()]
    phases += [("tx0", nx), ("ts0", 1), ("v1", ny // 2), ("v2", ny // 2), ("tx1", nx), ("ty1", ny), ("fa1", 1), ("fb1", 1)]
    phases += [(f"{name}s{k}", 0) for name in ("v1", "v2") for k in range(1, ny)]
    phases += [(f"{name}{t}", 1) for t in range(3) for name in ("s1", "s2")]
    phases += [("g0", nz), ("gz", 2), ("w0", 2), ("w1", 2), ("w2", 2)]
    phases += [(n, 1) for n in ("gp", "go", "ga", "gb", "l1", "l2", "r1", "w3")]
    for name, n in phases:
        plan[name] = (n_send, n_recv)
        n_send, n_recv = n_send + 1, n_recv + n
    part_rows = max(8, crops // 128)

    wrows = width + 2 * hb
    V = pltpu.VMEM
    scratch = [
        V((width, hb), BF16),
        V((hb, cols), BF16),
        V((width, ny // 2 * hb), BF16),
        V((ny // 2 * hb, cols), BF16),
        V((kp, cols), BF16),
        V((2, group, width), BF16),
        V((group, hb), F32),
        V((group, hb), BF16),
        V((2, group, cols), F32),
        V((2, npr, rb, cols), F32),
        V((2, nz, 2, 2, group // 2, cols), BF16),
        V((rb, cols), F32),
        V((rb, 1), F32),
        V((kp, crops), F32),
        V((kp, crops), F32),
        V((kp, 128), F32),
        V((16, crops), F32),
        V((8, crops), F32),
        V((3, 2 * part_rows, 128), F32),
        V((3, ndp, 2 * part_rows, 128), F32),
        V((3, 2 * part_rows, 128), F32),
        V((3, npr, 2 * part_rows, 128), F32),
        V((3, 2 * part_rows, 128), F32),
        V((kp, group), BF16),
        V((cols, kp), BF16),
        V((cols, group), F32),
        V((nz, 2, group // 2, cols), F32),
        V((nz, 2, group // 2, cols), F32),
        V((nz, 2, group // 2, cols), F32),
        V((2, nz - 1, group // 2, half), F32),
        V((npr, nz - 1, 2, rb // 2, half), F32),
        V((npr, 2, rb // 2, half), F32),
        V((2, group // 2, half), F32),
        V((npr, 2, rb // 2, half), F32),
        V((nz - 1, 2, rb // 2, half), F32),
        V((nz - 1, 2, rb // 2, half), F32),
        V((8, 128), F32),
        V((npr, 8, 128), F32),
        V((8, 128), F32),
        V((ndp, 8, 128), F32),
        V((group, cols), BF16),
        V((wrows, hb), F32),
        V((2, wrows // 4, hb), F32),
        V((2, nz, wrows // (2 * ndp), hb), F32),
        V((wrows, hb), F32),
        pltpu.SemaphoreType.DMA((n_send,)),
        pltpu.SemaphoreType.DMA((n_recv,)),
        pltpu.SemaphoreType.DMA((7,)),
    ]
    vmem = pl.BlockSpec(memory_space=pltpu.VMEM)
    gp, gw1, gw2, loss = pl.pallas_call(
        functools.partial(kernel, dims, plan),
        out_shape=(
            pltpu.VMEM((kp, cols), F32),
            pltpu.VMEM((width, hb), F32),
            pltpu.VMEM((hb, cols), F32),
            jax.ShapeDtypeStruct((1, 1), F32),
        ),
        in_specs=[pl.BlockSpec(memory_space=pl.ANY)] * 7,
        out_specs=(vmem,) * 4,
        scratch_shapes=scratch,
        compiler_params=pltpu.CompilerParams(
            collective_id=0, has_side_effects=True, vmem_limit_bytes=61 * 1024 * 1024
        ),
        cost_estimate=pl.CostEstimate(
            flops=8 * kp * crops * cols, bytes_accessed=4 * kp * cols * 4, transcendentals=2 * kp * crops
        ),
    )(s_in, t_in, w1s, w2s, w1t, w2t, protos)
    return gp, gw1, gw2, loss[0, 0]


def solution(mesh):
    ndp, npr = mesh.shape["dp"], mesh.shape["proto"]
    side = math.isqrt(npr)
    dims = dict(nz=ndp // 2, nx=side, ny=npr // side)
    both = P(("dp", "proto"), None)
    return jax.shard_map(
        functools.partial(step, dims),
        mesh=mesh,
        in_specs=(both, both, P(None, "proto"), P("proto", None), P(None, "proto"), P("proto", None), both),
        out_specs=(both, P(None, "proto"), P("proto", None), P()),
        check_vma=False,
    )
```

```python
import functools
import math

import jax
import jax.numpy as jnp
from jax import lax
from jax.experimental import pallas as pl
from jax.experimental.pallas import tpu as pltpu
from jax.sharding import PartitionSpec as P

MESH = pl.DeviceIdType.MESH
TEACHER_TEMP = 0.07
STUDENT_TEMP = 0.1
LOG2E = 1.4426950408889634
LN2 = 0.6931471805599453
F32 = jnp.float32
BF16 = jnp.bfloat16


def normal_cdf(x):
    return 0.5 * (1.0 + lax.erf(x * (1.0 / math.sqrt(2.0))))


def gelu(x):
    return x * normal_cdf(x)


def gelu_slope(x):
    return normal_cdf(x) + x * (jnp.exp(-0.5 * x * x) * (1.0 / math.sqrt(2.0 * math.pi)))


def nt_dot(a, b):
    return lax.dot_general(a, b, (((1,), (1,)), ((), ())), preferred_element_type=F32)


def tn_dot(a, b):
    return lax.dot_general(a, b, (((0,), (0,)), ((), ())), preferred_element_type=F32)


def unit_scale(raw):
    return lax.rsqrt(jnp.sum(raw * raw, axis=1, keepdims=True) + 1e-06)


def kernel(dims, plan, s_in, t_in, w1s_in, w2s_in, w1t_in, w2t_in, protos_in, gp_out, gw1_out, gw2_out, loss_out, *scratch):
    nz, nx, ny, rb, q = dims["nz"], dims["nx"], dims["ny"], dims["rb"], dims["q"]
    ndp, npr = 2 * nz, nx * ny
    width, hb, cols, kp = w1s_in.shape[0], w1s_in.shape[1], w2s_in.shape[1], protos_in.shape[0]
    group = rb * npr
    crops = group * ndp
    total_protos = kp * ndp * npr
    tiles = crops // 128
    part_rows = max(8, tiles)
    half = cols // 2
    hr = rb // 2
    (w1s, w2s, w1g, w2g, protos, tok, pre_s, hid_s, rawp, rawr, units, own_float, own_scale, ex, lg2, colb, wb, rows8,
     ps1, psa, psb, psbr, psc, gt, ptr, ugt, sibs, sibr, part, zrecv, precv, ohr, a2, a2r, b2, b2r, losst, lossr, lossd,
     lossdr, rg, gw, gwr, gwz, fw, ssem, rsem, lsem) = scratch

    dp, me = lax.axis_index("dp"), lax.axis_index("proto")
    z, c = dp // 2, dp % 2
    x, y = me // ny, me % ny

    def started(src, dst, name, to_dp, to_proto, nth=0, send_as=None):
        s, r = plan[send_as or name][0], plan[name][1]
        pltpu.make_async_remote_copy(
            src_ref=src, dst_ref=dst, send_sem=ssem.at[s], recv_sem=rsem.at[r + nth],
            device_id=(to_dp, to_proto), device_id_type=MESH,
        ).start()

    def arrived(dst, name, nth=0):
        pltpu.make_async_copy(dst, dst, rsem.at[plan[name][1] + nth]).wait()

    def gone(src, name):
        pltpu.make_async_copy(src, src, ssem.at[plan[name][0]]).wait()

    def loop(lo, hi, fn, unroll=None):
        if unroll is None:
            for k in range(lo, hi):
                fn(k)
            return

        def step(k, carry):
            fn(k)
            return carry

        lax.fori_loop(lo, hi, step, 0, unroll=unroll)

    def proto_of(xx, yy):
        return lax.rem(xx + nx, nx) * ny + lax.rem(yy + ny, ny)

    def rows(p):
        return pl.ds(pl.multiple_of(p * rb, rb), rb)

    def hrows(p):
        return pl.ds(pl.multiple_of(p * hr, hr), hr)

    def ring(value, n):
        return lax.rem(value + n, n)

    left, right = pl.ds(0, width // 2), pl.ds(width // 2, width // 2)
    lo, hi = pl.ds(0, half), pl.ds(half, half)
    sib = dp + 1 - 2 * c

    ny2 = ny // 2

    def w1_slot(s):
        return w1g.at[:, pl.ds(pl.multiple_of(s * hb, hb), hb)]

    def w2_slot(s):
        return w2g.at[pl.ds(pl.multiple_of(s * hb, hb), hb)]

    loads = [
        pltpu.make_async_copy(src, dst, lsem.at[n])
        for n, (src, dst) in enumerate(
            [(t_in, tok.at[0, rows(c * nx + x)]), (s_in, tok.at[1, rows(me)]), (w1t_in, w1_slot(lax.rem(y, ny2))),
             (w2t_in, w2_slot(lax.rem(y, ny2))), (protos_in, protos), (w1s_in, w1s), (w2s_in, w2s)]
        )
    ]
    for n, load in enumerate(loads):
        if n not in (2, 3):
            load.start()

    @pl.when(y // ny2 == c)
    def _():
        loads[2].start()
        loads[3].start()

    barrier = pltpu.get_barrier_semaphore()

    def greet_proto(k):
        pl.semaphore_signal(barrier, inc=1, device_id=(dp, ring(me + k, npr)), device_id_type=MESH)

    def greet_dp(k):
        pl.semaphore_signal(barrier, inc=1, device_id=(ring(dp + k, ndp), me), device_id_type=MESH)

    loop(1, npr, greet_proto)
    loop(1, ndp, greet_dp)
    loads[0].wait()
    loads[1].wait()
    pl.semaphore_wait(barrier, npr - 1 + ndp - 1)

    def front_start():
        mine = tok.at[0, rows(c * nx + x)]
        for k in range(1, nx):
            started(mine, mine, "tx0", dp, proto_of(x + k, y), k)
        started(mine, mine, "ts0", sib, me)

        @pl.when(y // ny2 == c)
        def _():
            s = lax.rem(y, ny2)
            loads[2].wait()
            for k in range(1, ny):
                started(w1_slot(s), w1_slot(s), "v1", dp, proto_of(x, y + k), s, f"v1s{k}")
            loads[3].wait()
            for k in range(1, ny):
                started(w2_slot(s), w2_slot(s), "v2", dp, proto_of(x, y + k), s, f"v2s{k}")

    def front_forward():
        for k in range(1, nx):
            block = tok.at[0, rows(c * nx + lax.rem(x - k + nx, nx))]
            arrived(block, "tx0", k)
            started(block, block, "ts0", sib, me)

    def front_wait():
        arrived(tok.at[0, pl.ds(pl.multiple_of((1 - c) * (nx * rb), nx * rb), nx * rb)], "ts0")
        for s in range(ny2):

            @pl.when(c * ny2 + s != y)
            def _(s=s):
                arrived(w1_slot(s), "v1", s)
                arrived(w2_slot(s), "v2", s)

    def front_drain():
        gone(tok.at[0, pl.ds(0, (nx - 1) * rb)], "tx0")
        gone(tok.at[0, pl.ds(0, nx * rb)], "ts0")

        @pl.when(y // ny2 == c)
        def _():
            for k in range(1, ny):
                gone(w1_slot(0), f"v1s{k}")
                gone(w2_slot(0), f"v2s{k}")

    def front_head():
        r = pl.ds(0, 2 * nx * rb)
        pre = jnp.dot(tok[0, r, :], w1g[...], preferred_element_type=F32)
        rawp[0, r, :] = jnp.dot(gelu(pre).astype(BF16), w2g[...], preferred_element_type=F32)

    def front_raw_send():
        for kc in range(2):
            for kx in range(nx):
                if kc or kx:
                    cc, xx = c + kc - 2 * c * kc, lax.rem(x + kx, nx)
                    started(rawp.at[0, rows(cc * nx + xx)], rawr.at[0, kc * nx + kx], "rr0", 2 * z + cc, proto_of(xx, y))

    def front_raw_finish():
        arrived(rawr.at[0, pl.ds(1, 2 * nx - 1)], "rr0")
        raw = rawp[0, rows(c * nx + x), :]
        for k in range(1, 2 * nx):
            raw = raw + rawr[0, k]
        put_unit(0, raw)

    def front_raw_drain():
        gone(rawr.at[0, pl.ds(1, 2 * nx - 1)], "rr0")

    def put_unit(v, raw):
        scale = unit_scale(raw)
        unit_float = raw * scale
        if v == 1:
            own_float[...] = unit_float
            own_scale[...] = scale
        units[v, z, c, :, hrows(me), :] = unit_float.astype(BF16).reshape(2, hr, cols)

    def tokens_start_x(v):
        mine = tok.at[v, rows(me)]
        for k in range(1, nx):
            started(mine, mine, f"tx{v}", dp, proto_of(x + k, y), k)

    def tokens_start_y(v):
        mine = tok.at[v, rows(me)]
        for k in range(1, ny):
            started(mine, mine, f"ty{v}", dp, proto_of(x, y + k), k)

    def tokens_forward_y(v):
        for k in range(1, nx):
            block = rows(proto_of(x - k, y))
            arrived(tok.at[v, block], f"tx{v}", k)
            ref = tok.at[v, block, left]
            for m in range(1, ny):
                started(ref, ref, f"fa{v}", dp, proto_of(x, y + m))

    def tokens_forward_x(v):
        for k in range(1, ny):
            block = rows(proto_of(x, y - k))
            arrived(tok.at[v, block], f"ty{v}", k)
            ref = tok.at[v, block, right]
            for m in range(1, nx):
                started(ref, ref, f"fb{v}", dp, proto_of(x + m, y))

    diagonal = pl.ds(0, (nx - 1) * (ny - 1) * rb)

    def tokens_wait(v):
        arrived(tok.at[v, diagonal, left], f"fa{v}")
        arrived(tok.at[v, diagonal, right], f"fb{v}")

    def tokens_drain(v):
        gone(tok.at[v, pl.ds(0, (nx - 1) * rb)], f"tx{v}")
        gone(tok.at[v, pl.ds(0, (ny - 1) * rb)], f"ty{v}")
        gone(tok.at[v, diagonal, left], f"fa{v}")
        gone(tok.at[v, diagonal, right], f"fb{v}")

    def head(v):
        step = min(group, 256)

        def chunk(i):
            r = pl.ds(pl.multiple_of(i * step, step), step)
            pre = jnp.dot(tok[v, r, :], w1s[...], preferred_element_type=F32)
            hidden = gelu(pre).astype(BF16)
            pre_s[r, :] = pre
            hid_s[r, :] = hidden
            rawp[v, r, :] = jnp.dot(hidden, w2s[...], preferred_element_type=F32)

        loop(0, group // step, chunk, unroll=group // step)

    def raw_send(v):
        def send(k):
            to = ring(me + k, npr)
            started(rawp.at[v, rows(to)], rawr.at[v, k], f"rr{v}", dp, to)

        loop(1, npr, send)

    others = pl.ds(1, npr - 1)

    def raw_finish(v):
        arrived(rawr.at[v, others], f"rr{v}")
        raw = rawp[v, rows(me), :]
        for k in range(1, npr):
            raw = raw + rawr[v, k]
        put_unit(v, raw)

    def raw_drain(v):
        gone(rawr.at[v, others], f"rr{v}")

    def band(xx):
        return pl.ds(pl.multiple_of(ring(xx, nx) * (ny * hr), ny * hr), ny * hr)

    def ag_first(v):
        mine = units.at[v, z, c, 1, hrows(me)]
        for k in range(1, nz):
            started(mine.at[:, hi], mine.at[:, hi], f"b1{v}", ring(z + k, nz) * 2 + c, me)
        loop(1, npr, lambda k: started(mine.at[:, lo], mine.at[:, lo], f"a1{v}", dp, ring(me + k, npr)))
        direct = units.at[v, z, c, 0, hrows(me)]
        for kz in list(range(1, nz)) + [0]:

            def send(k, kz=kz):
                started(direct, direct, f"d1{v}", ring(z + kz, nz) * 2 + c, ring(me + k, npr), kz)

            loop(0 if kz else 1, npr, send)

    def ag_second(v):
        arrived(units.at[v, pl.ds(0, nz - 1), c, 1, hrows(me), hi], f"b1{v}")
        col = units.at[v, :, c, 1, hrows(me), hi]
        for kx in range(nx):
            for ky in range(ny):
                if kx or ky:
                    started(col, col, f"b2{v}", dp, proto_of(x + kx, y + ky), kx)
        arrived(units.at[v, z, c, 1, pl.ds(0, (npr - 1) * hr), lo], f"a1{v}")
        plane = units.at[v, z, c, 1, :, lo]
        for k in range(1, nz):
            started(plane, plane, f"a2{v}", ring(z + k, nz) * 2 + c, me, k)
        started(plane, plane, f"sa{v}", sib, me)

    def ag_third(v):
        for k in range(nz):
            plane = units.at[v, ring(z - k, nz), c, 0]
            if k:
                arrived(plane, f"d1{v}", k)
            else:
                arrived(units.at[v, z, c, 0, pl.ds(0, (npr - 1) * hr)], f"d1{v}", k)
            started(plane, plane, f"sd{v}", sib, me)

    def ag_fourth(v):
        for k in range(1, nz):
            plane = units.at[v, ring(z - k, nz), c, 1, :, lo]
            arrived(plane, f"a2{v}", k)
            started(plane, plane, f"sa{v}", sib, me)
        for k in range(nx):
            piece = units.at[v, :, c, 1, band(x - k), hi]
            if k:
                arrived(piece, f"b2{v}", k)
            else:
                arrived(units.at[v, :, c, 1, pl.ds(0, (ny - 1) * hr), hi], f"b2{v}", k)
            started(piece, piece, f"sb{v}", sib, me)

    def ag_wait_straight(v):
        arrived(units.at[v, :, 1 - c, 0], f"sd{v}")

    def ag_wait(v):
        arrived(units.at[v, :, 1 - c, 1, :, lo], f"sa{v}")
        arrived(units.at[v, :, 1 - c, 1, :, hi], f"sb{v}")

    def ag_drain(v):
        gone(protos.at[pl.ds(0, (nz * npr - 1) * hr)], f"d1{v}")
        gone(units.at[v, :, c, 0], f"sd{v}")
        gone(units.at[v, z, c, 1, pl.ds(0, (npr - 1) * hr), lo], f"a1{v}")
        gone(units.at[v, pl.ds(0, nz - 1), c, 1, hrows(me), hi], f"b1{v}")
        gone(units.at[v, :, c, 1, pl.ds(0, (npr - 1) * hr), hi], f"b2{v}")
        gone(units.at[v, pl.ds(0, nz - 1), c, 1, :, lo], f"a2{v}")
        gone(units.at[v, :, c, 1, :, lo], f"sa{v}")
        gone(units.at[v, :, c, 1, :, hi], f"sb{v}")

    def slow_first(v):
        mine = units.at[v, z, c, :, hrows(me)]
        for k in range(1, nz):
            started(mine.at[:, :, hi], mine.at[:, :, hi], f"b1{v}", ring(z + k, nz) * 2 + c, me)
        loop(1, npr, lambda k: started(mine.at[:, :, lo], mine.at[:, :, lo], f"a1{v}", dp, ring(me + k, npr)))

    def slow_second_z(v):
        arrived(units.at[v, z, c, :, pl.ds(0, (npr - 1) * hr), lo], f"a1{v}")
        plane = units.at[v, z, c, :, :, lo]
        for k in range(1, nz):
            started(plane, plane, f"a2{v}", ring(z + k, nz) * 2 + c, me, k)
        started(plane, plane, f"sa{v}", sib, me)

    def slow_second_proto(v):
        arrived(units.at[v, pl.ds(0, nz - 1), c, :, hrows(me), hi], f"b1{v}")
        col = units.at[v, :, c, :, hrows(me), hi]
        for kx in range(nx):
            for ky in range(ny):
                if kx or ky:
                    started(col, col, f"b2{v}", dp, proto_of(x + kx, y + ky), kx)

    def slow_third(v):
        for k in range(1, nz):
            plane = units.at[v, ring(z - k, nz), c, :, :, lo]
            arrived(plane, f"a2{v}", k)
            started(plane, plane, f"sa{v}", sib, me)
        for k in range(nx):
            piece = units.at[v, :, c, :, band(x - k), hi]
            if k:
                arrived(piece, f"b2{v}", k)
            else:
                arrived(units.at[v, :, c, :, pl.ds(0, (ny - 1) * hr), hi], f"b2{v}", k)
            started(piece, piece, f"sb{v}", sib, me)

    def slow_wait(v):
        arrived(units.at[v, :, 1 - c, :, :, lo], f"sa{v}")
        arrived(units.at[v, :, 1 - c, :, :, hi], f"sb{v}")

    def slow_drain(v):
        gone(units.at[v, z, c, :, pl.ds(0, (npr - 1) * hr), lo], f"a1{v}")
        gone(units.at[v, pl.ds(0, nz - 1), c, :, hrows(me), hi], f"b1{v}")
        gone(units.at[v, :, c, :, pl.ds(0, (npr - 1) * hr), hi], f"b2{v}")
        gone(units.at[v, pl.ds(0, nz - 1), c, :, :, lo], f"a2{v}")
        gone(units.at[v, :, c, :, :, lo], f"sa{v}")
        gone(units.at[v, :, c, :, :, hi], f"sb{v}")

    pb = min(kp, 256)
    nb = kp // pb
    gtiles = group // 128

    def teacher_scores(cc, h):
        wide = group // 2

        def step(i):
            zz, b = i // nb, i % nb
            r = pl.ds(pl.multiple_of(b * pb, pb), pb)
            s = nt_dot(protos[r, :], units[0, zz, cc, h])
            e = jnp.exp2(s * (LOG2E / TEACHER_TEMP))
            ex[r, pl.ds(pl.multiple_of((2 * zz + cc) * group + h * wide, wide), wide)] = e
            acc = e[:, :128]
            for j in range(1, wide // 128):
                acc = acc + e[:, j * 128 : (j + 1) * 128]
            colb[r, :] += acc

        loop(0, nz * nb, step, unroll=4 * nb)

    def first_scales():
        def scale(i):
            r = pl.ds(pl.multiple_of(i * 64, 64), 64)
            total = jnp.sum(colb[r, :], axis=1, keepdims=True)
            colb[r, :] = jnp.broadcast_to(1.0 / (total_protos * total), (64, 128))

        loop(0, kp // 64, scale, unroll=2)

    def student_scores(cc):
        def step(i):
            zz, b = i // nb, i % nb
            r = pl.ds(pl.multiple_of(b * pb, pb), pb)
            lanes = pl.ds(pl.multiple_of((2 * zz + cc) * group, group), group)
            s = nt_dot(protos[r, :], units[1, zz, cc].reshape(group, cols)) * (LOG2E / STUDENT_TEMP)
            lg2[r, lanes] = s
            rows8[:, lanes] += jnp.sum(jnp.exp2(s).reshape(pb // 8, 8, group), axis=0)

        loop(0, nz * nb, step, unroll=2 * nb)

    def row_pass(fresh):
        rows8[...] = jnp.zeros_like(rows8)

        def step(i):
            base = pl.multiple_of(i * 64, 64)
            if fresh:
                accs = [None] * 8
                for j in range(tiles):
                    lanes = slice(j * 128, (j + 1) * 128)
                    w = wb[0:8, lanes]
                    for a in range(8):
                        term = ex[pl.ds(base + 8 * a, 8), lanes] * w
                        accs[a] = term if accs[a] is None else accs[a] + term
                scales = []
                for a in range(8):
                    total = jnp.sum(accs[a], axis=1, keepdims=True)
                    scale = jnp.broadcast_to(1.0 / (total_protos * total), (8, 128))
                    colb[pl.ds(base + 8 * a, 8), :] = scale
                    scales.append(scale)
            else:
                scales = [colb[pl.ds(base + 8 * a, 8), :] for a in range(8)]
            for j in range(tiles):
                lanes = slice(j * 128, (j + 1) * 128)
                terms = [ex[pl.ds(base + 8 * a, 8), lanes] * scales[a] for a in range(8)]
                while len(terms) > 1:
                    terms = [terms[n] + terms[n + 1] for n in range(0, len(terms), 2)]
                rows8[:, lanes] += terms[0]

        loop(0, kp // 64, step, unroll=2)

    def put_rows(t, at):
        for j in range(tiles):
            ps1[t, at * part_rows + j : at * part_rows + j + 1, :] = jnp.sum(
                rows8[:, j * 128 : (j + 1) * 128], axis=0, keepdims=True
            )

    def span(t):
        return pl.ds(0, part_rows * (2 if t == 2 else 1))

    def sum_send(t):
        for k in range(1, ndp):
            started(ps1.at[t, span(t)], psa.at[t, k, span(t)], f"s1{t}", ring(dp + k, ndp), me)

    def sum_middle(t):
        arrived(psa.at[t, pl.ds(1, ndp - 1), span(t)], f"s1{t}")
        total = ps1[t, span(t), :]
        for k in range(1, ndp):
            total = total + psa[t, k, span(t), :]
        psb[t, span(t), :] = total
        for k in range(1, npr):
            started(psb.at[t, span(t)], psbr.at[t, k, span(t)], f"s2{t}", dp, ring(me + k, npr))

    def sum_finish(t):
        arrived(psbr.at[t, others, span(t)], f"s2{t}")
        total = psb[t, span(t), :]
        for k in range(1, npr):
            total = total + psbr[t, k, span(t), :]
        psc[t, span(t), :] = total

    def sum_drain(t):
        gone(psa.at[t, pl.ds(1, ndp - 1), span(t)], f"s1{t}")
        gone(psbr.at[t, others, span(t)], f"s2{t}")

    def spread(t, at, fn, slot):
        for j in range(tiles):
            v = fn(psc[t, at * part_rows + j : at * part_rows + j + 1, :])
            wb[pl.ds(8 * slot, 8), j * 128 : (j + 1) * 128] = jnp.broadcast_to(v, (8, 128))

    def next_weight(v):
        return 1.0 / (crops * v)

    front_start()
    tokens_start_x(1)
    tokens_start_y(1)
    ps1[...] = jnp.zeros_like(ps1)
    colb[...] = jnp.zeros_like(colb)
    for load in loads[4:]:
        load.wait()
    front_forward()
    ptr[...] = protos[...].astype(F32).T.astype(BF16)
    front_wait()
    front_head()
    front_raw_send()
    tokens_forward_y(1)
    tokens_forward_x(1)
    front_raw_finish()
    ag_first(0)
    ag_second(0)
    tokens_wait(1)
    head(1)
    ag_third(0)
    teacher_scores(c, 0)
    ag_fourth(0)
    raw_send(1)
    ag_wait_straight(0)
    teacher_scores(1 - c, 0)
    teacher_scores(c, 1)
    ag_wait(0)
    teacher_scores(1 - c, 1)
    first_scales()
    row_pass(False)
    put_rows(0, 0)
    sum_send(0)
    raw_finish(1)
    slow_first(1)
    sum_middle(0)
    slow_second_z(1)
    sum_finish(0)
    spread(0, 0, next_weight, 0)
    slow_second_proto(1)
    row_pass(True)
    put_rows(1, 0)
    sum_send(1)
    sum_middle(1)
    slow_third(1)
    rows8[...] = jnp.zeros_like(rows8)
    student_scores(c)
    slow_wait(1)
    student_scores(1 - c)
    put_rows(2, 1)
    sum_finish(1)
    spread(1, 0, next_weight, 0)
    row_pass(True)
    put_rows(2, 0)
    sum_send(2)
    sum_middle(2)
    sum_finish(2)
    spread(2, 0, lambda v: 1.0 / v, 0)
    spread(2, 1, lambda v: jnp.log(v) * LOG2E, 1)

    gp_out[...] = jnp.zeros_like(gp_out)
    losst[...] = jnp.zeros_like(losst)
    share = 1.0 / (crops * STUDENT_TEMP)

    def group_grads(zz, cc):
        lane0 = pl.multiple_of((zz * 2 + cc) * group, group)
        u = units[1, zz, cc].reshape(group, cols)

        def step(b):
            base = pl.multiple_of(b * pb, pb)
            r = pl.ds(base, pb)
            lanes = [pl.ds(pl.multiple_of(lane0 + j * 128, 128), 128) for j in range(gtiles)]
            inv = [wb[0:8, l] for l in lanes]
            norm = [wb[8:16, l] for l in lanes]
            lossa = [jnp.zeros((8, 128), F32) for _ in range(2 * gtiles)]
            for a in range(0, pb, 16):
                scale = [colb[pl.ds(base + a + h, 8), :] for h in (0, 8)]
                for j in range(gtiles):
                    outs = []
                    for h in range(2):
                        rr = pl.ds(base + a + 8 * h, 8)
                        tgt = ex[rr, lanes[j]] * scale[h] * inv[j]
                        rel = lg2[rr, lanes[j]] - norm[j]
                        lossa[2 * j + h] = lossa[2 * j + h] - tgt * rel
                        outs.append((jnp.exp2(rel) - tgt) * share)
                    gt[pl.ds(base + a, 16), j * 128 : (j + 1) * 128] = jnp.concatenate(outs, axis=0).astype(BF16)
            total = lossa[0]
            for term in lossa[1:]:
                total = total + term
            losst[...] += total
            gp_out[r, :] += jnp.dot(gt[r, :], u, preferred_element_type=F32)

        loop(0, nb, step, unroll=nb)
        ugt[...] = jnp.dot(ptr[...], gt[...], preferred_element_type=F32)
        return ugt[...].T.reshape(2, group // 2, cols)

    planes = sorted(range(1, nz), key=lambda k: -min(k, nz - k)) + [0]
    for n, k in enumerate(planes):
        zz = ring(z + k, nz)
        sibs[n] = group_grads(zz, 1 - c)
        started(sibs.at[n], sibr.at[n], "g0", sib, me, n)
        mine = group_grads(zz, c)
        arrived(sibr.at[n], "g0", n)
        part[k] = mine + sibr[n]
        if k:
            for h in range(2):
                started(part.at[k, h, :, lo], zrecv.at[h, k - 1], "gz", zz * 2 + c, me, h)

        def send(m, k=k):
            to = ring(me + m, npr)
            if k:
                started(part.at[k, :, hrows(to), hi], precv.at[m, k - 1], "gp", dp, to)
            else:
                started(part.at[k, :, hrows(to), hi], ohr.at[m], "go", dp, to)

        loop(1, npr, send)

    for h in range(2):
        arrived(zrecv.at[h], "gz", h)
        total = part[0, h, :, lo]
        for k in range(nz - 1):
            total = total + zrecv[h, k]
        a2[h] = total

        def send(k, h=h):
            to = ring(me + k, npr)
            started(a2.at[h, hrows(to)], a2r.at[k, h], "ga", dp, to)

        loop(1, npr, send)
        if h == 0:
            arrived(precv.at[others], "gp")
            total = part[pl.ds(1, nz - 1), :, hrows(me), hi]
            for k in range(1, npr):
                total = total + precv[k]
            b2[...] = total
            for k in range(1, nz):
                started(b2.at[k - 1], b2r.at[k - 1], "gb", ring(z + k, nz) * 2 + c, me)

    losst[...] = losst[...] * (LN2 / crops)
    loop(1, npr, lambda k: started(losst, lossr.at[k], "l1", dp, ring(me + k, npr)))

    arrived(ohr.at[others], "go")
    grad_hi = part[0, :, hrows(me), hi]
    for k in range(1, npr):
        grad_hi = grad_hi + ohr[k]
    arrived(b2r, "gb")
    for k in range(nz - 1):
        grad_hi = grad_hi + b2r[k]
    arrived(a2r.at[others], "ga")
    grad_lo = a2[:, hrows(me), :]
    for k in range(1, npr):
        grad_lo = grad_lo + a2r[k]

    unit_grad = jnp.concatenate([grad_lo.reshape(rb, half), grad_hi.reshape(rb, half)], axis=1)
    own = own_float[...]
    along = jnp.sum(own * unit_grad, axis=1, keepdims=True)
    rg[rows(me), :] = ((unit_grad - own * along) * own_scale[...]).astype(BF16)
    loop(1, npr, lambda k: started(rg.at[rows(me)], rg.at[rows(me)], "r1", dp, ring(me + k, npr)))

    arrived(lossr.at[others], "l1")
    total = losst[...]
    for k in range(1, npr):
        total = total + lossr[k]
    lossd[...] = total
    loop(1, ndp, lambda k: started(lossd, lossdr.at[k], "l2", ring(dp + k, ndp), me))
    pre_s[...] = gelu_slope(pre_s[...])

    arrived(rg.at[pl.ds(0, (npr - 1) * rb)], "r1")
    raw_grad = rg[...]
    pre_grad = (nt_dot(raw_grad, w2s[...]) * pre_s[...]).astype(BF16)
    whole = gw.shape[0]
    parts = 2
    share_rows, piece = whole // (2 * parts), whole // (ndp * parts)

    def half_of(n, cc):
        return pl.ds(pl.multiple_of((2 * n + cc) * share_rows, 8), share_rows)

    def piece_of(n, zz):
        return pl.ds(pl.multiple_of((2 * n + c) * share_rows + zz * piece, 8), piece)

    wchunk = min(width, 256)
    sent = 0
    for i in range(width // wchunk + 1):
        if i < width // wchunk:
            sl = slice(i * wchunk, (i + 1) * wchunk)
            gw[sl, :] = tn_dot(tok[1, :, sl], pre_grad)
            done = (i + 1) * wchunk
        else:
            grad2 = tn_dot(hid_s[...], raw_grad)
            gw[pl.ds(width, hb), :] = grad2[:, :hb]
            gw[pl.ds(width + hb, hb), :] = grad2[:, hb:]
            done = whole
        while sent < parts and done >= 2 * (sent + 1) * share_rows:
            started(gw.at[half_of(sent, 1 - c)], gwr.at[sent], "w0", sib, me, sent)
            sent += 1

    zpeers = pl.ds(1, nz - 1)
    for n in range(parts):
        arrived(gwr.at[n], "w0", n)
        gw[half_of(n, c), :] += gwr[n]
        for k in range(1, nz):
            zz = ring(z + k, nz)
            started(gw.at[piece_of(n, zz)], gwz.at[n, k], "w1", zz * 2 + c, me, n)
    for n in range(parts):
        total = gw[piece_of(n, z), :]
        arrived(gwz.at[n, zpeers], "w1", n)
        for k in range(1, nz):
            total = total + gwz[n, k]
        fw[piece_of(n, z), :] = total
        for k in range(1, nz):
            started(fw.at[piece_of(n, z)], fw.at[piece_of(n, z)], "w2", ring(z + k, nz) * 2 + c, me, n)
    for n in range(parts):
        arrived(gwz.at[n, zpeers], "w2", n)
        started(fw.at[half_of(n, c)], fw.at[half_of(n, c)], "w3", sib, me)

    arrived(lossdr.at[pl.ds(1, ndp - 1)], "l2")
    loss = lossd[...]
    for k in range(1, ndp):
        loss = loss + lossdr[k]
    loss_out[...] = jnp.sum(jnp.sum(loss, axis=0, keepdims=True), axis=1, keepdims=True)

    front_drain()
    front_raw_drain()
    tokens_drain(1)
    raw_drain(1)
    ag_drain(0)
    slow_drain(1)
    for t in range(3):
        sum_drain(t)
    gone(sibs, "g0")
    gone(zrecv, "gz")
    gone(ohr.at[others], "go")
    gone(precv.at[others], "gp")
    gone(a2r.at[others], "ga")
    gone(b2r, "gb")
    gone(lossr.at[others], "l1")
    gone(lossdr.at[pl.ds(1, ndp - 1)], "l2")
    gone(rg.at[pl.ds(0, (npr - 1) * rb)], "r1")
    gone(gwr, "w0")
    gone(gwz.at[:, zpeers], "w1")
    gone(gwz.at[:, zpeers], "w2")

    arrived(gwr, "w3")
    gw1_out[...] = fw[:width, :]
    gw2_out[:, :hb] = fw[width : width + hb, :]
    gw2_out[:, hb:] = fw[width + hb :, :]
    gone(gwr, "w3")


def copy_kernel(*refs):
    n = len(refs) // 2
    copies = [pltpu.make_async_copy(refs[i], refs[n + i], refs[-1].at[i]) for i in range(n)]
    for copy in copies:
        copy.start()
    for copy in copies:
        copy.wait()


def write_out(*arrays):
    anywhere = pl.BlockSpec(memory_space=pl.ANY)
    return pl.pallas_call(
        copy_kernel,
        out_shape=tuple(jax.ShapeDtypeStruct(a.shape, a.dtype) for a in arrays),
        in_specs=[anywhere] * len(arrays),
        out_specs=(anywhere,) * len(arrays),
        scratch_shapes=[pltpu.SemaphoreType.DMA((len(arrays),))],
        cost_estimate=pl.CostEstimate(flops=0, bytes_accessed=8 * sum(a.size for a in arrays), transcendentals=0),
    )(*arrays)


def step(dims, s_in, t_in, w1s, w2s, w1t, w2t, protos):
    nz, nx, ny = dims["nz"], dims["nx"], dims["ny"]
    ndp, npr = 2 * nz, nx * ny
    rb, width = s_in.shape
    hb, cols = w2s.shape
    kp = protos.shape[0]
    group = rb * npr
    crops = group * ndp
    half = cols // 2
    dims = dict(dims, rb=rb, q=group // 128)

    plan, n_send, n_recv = {}, 0, 0
    phases = [(f"{name}{v}", n) for v in (0, 1) for name, n in dict(
        rr=1, a1=1, b1=1, b2=nx, a2=nz, d1=nz, sa=1, sb=1, sd=1).items()]
    phases += [("tx0", nx), ("ts0", 1), ("v1", ny // 2), ("v2", ny // 2), ("tx1", nx), ("ty1", ny), ("fa1", 1), ("fb1", 1)]
    phases += [(f"{name}s{k}", 0) for name in ("v1", "v2") for k in range(1, ny)]
    phases += [(f"{name}{t}", 1) for t in range(3) for name in ("s1", "s2")]
    phases += [("g0", nz), ("gz", 2), ("w0", 2), ("w1", 2), ("w2", 2)]
    phases += [(n, 1) for n in ("gp", "go", "ga", "gb", "l1", "l2", "r1", "w3")]
    for name, n in phases:
        plan[name] = (n_send, n_recv)
        n_send, n_recv = n_send + 1, n_recv + n
    part_rows = max(8, crops // 128)

    wrows = width + 2 * hb
    V = pltpu.VMEM
    scratch = [
        V((width, hb), BF16),
        V((hb, cols), BF16),
        V((width, ny // 2 * hb), BF16),
        V((ny // 2 * hb, cols), BF16),
        V((kp, cols), BF16),
        V((2, group, width), BF16),
        V((group, hb), F32),
        V((group, hb), BF16),
        V((2, group, cols), F32),
        V((2, npr, rb, cols), F32),
        V((2, nz, 2, 2, group // 2, cols), BF16),
        V((rb, cols), F32),
        V((rb, 1), F32),
        V((kp, crops), F32),
        V((kp, crops), F32),
        V((kp, 128), F32),
        V((16, crops), F32),
        V((8, crops), F32),
        V((3, 2 * part_rows, 128), F32),
        V((3, ndp, 2 * part_rows, 128), F32),
        V((3, 2 * part_rows, 128), F32),
        V((3, npr, 2 * part_rows, 128), F32),
        V((3, 2 * part_rows, 128), F32),
        V((kp, group), BF16),
        V((cols, kp), BF16),
        V((cols, group), F32),
        V((nz, 2, group // 2, cols), F32),
        V((nz, 2, group // 2, cols), F32),
        V((nz, 2, group // 2, cols), F32),
        V((2, nz - 1, group // 2, half), F32),
        V((npr, nz - 1, 2, rb // 2, half), F32),
        V((npr, 2, rb // 2, half), F32),
        V((2, group // 2, half), F32),
        V((npr, 2, rb // 2, half), F32),
        V((nz - 1, 2, rb // 2, half), F32),
        V((nz - 1, 2, rb // 2, half), F32),
        V((8, 128), F32),
        V((npr, 8, 128), F32),
        V((8, 128), F32),
        V((ndp, 8, 128), F32),
        V((group, cols), BF16),
        V((wrows, hb), F32),
        V((2, wrows // 4, hb), F32),
        V((2, nz, wrows // (2 * ndp), hb), F32),
        V((wrows, hb), F32),
        pltpu.SemaphoreType.DMA((n_send,)),
        pltpu.SemaphoreType.DMA((n_recv,)),
        pltpu.SemaphoreType.DMA((7,)),
    ]
    vmem = pl.BlockSpec(memory_space=pltpu.VMEM)
    gp, gw1, gw2, loss = pl.pallas_call(
        functools.partial(kernel, dims, plan),
        out_shape=(
            pltpu.VMEM((kp, cols), F32),
            pltpu.VMEM((width, hb), F32),
            pltpu.VMEM((hb, cols), F32),
            jax.ShapeDtypeStruct((1, 1), F32),
        ),
        in_specs=[pl.BlockSpec(memory_space=pl.ANY)] * 7,
        out_specs=(vmem,) * 4,
        scratch_shapes=scratch,
        compiler_params=pltpu.CompilerParams(
            collective_id=0, has_side_effects=True, vmem_limit_bytes=61 * 1024 * 1024
        ),
        cost_estimate=pl.CostEstimate(
            flops=8 * kp * crops * cols, bytes_accessed=4 * kp * cols * 4, transcendentals=2 * kp * crops
        ),
    )(s_in, t_in, w1s, w2s, w1t, w2t, protos)
    gp, gw1, gw2 = write_out(gp, gw1, gw2)
    return gp, gw1, gw2, loss[0, 0]


def solution(mesh):
    ndp, npr = mesh.shape["dp"], mesh.shape["proto"]
    side = math.isqrt(npr)
    dims = dict(nz=ndp // 2, nx=side, ny=npr // side)
    both = P(("dp", "proto"), None)
    return jax.shard_map(
        functools.partial(step, dims),
        mesh=mesh,
        in_specs=(both, both, P(None, "proto"), P("proto", None), P(None, "proto"), P("proto", None), both),
        out_specs=(both, P(None, "proto"), P("proto", None), P()),
        check_vma=False,
    )
```
